32 devices in a mesh: groups: 2 (over y), strip: 4 (over z), cand: 2 (over x), feat: 2 (over core).
Axes of the slice: x: 2, y: 2, z: 4, core: 2. Of those that a mesh axis runs over, the one named last changes fastest.
Arguments:
- src_pos: float32 [3, 32768], P(None, ('groups', 'strip')), parts along dimension 1, may hold values from -1 to 1
- src_feat: bfloat16 [128, 32768], P('feat', ('groups', 'strip')), parts along dimension 1, may hold values from -10.5 to 10.5
- tgt_pos: float32 [3, 32768], P(None, ('groups', 'strip', 'cand')), parts along dimension 1, may hold values from -0.6 to 1.4
- tgt_feat: bfloat16 [128, 32768], P('feat', ('groups', 'strip', 'cand')), parts along dimension 1, may hold values from -10.5 to 10.5
- displacement: float32 [3, 32768], P(None, ('groups', 'strip')), parts along dimension 1, may hold values from -1 to 1
- sigma_sq: float32 [8], P(('groups', 'strip')), parts along dimension 0, may hold values from 0.5 to 2
- seed_target: int32 [32768], P(('groups', 'strip')), parts along dimension 0, may hold values from 0 to 8191
- counts: int32 [8], P(('groups', 'strip')), parts along dimension 0, may hold values from 512 to 4096
- edges: int32 [8, 32768], P(None, ('groups', 'strip')), parts along dimension 1, may hold values from 0 to 12287, as said below
Outputs:
- new_disp: float32 [3, 32768], P(None, ('groups', 'strip')), parts along dimension 1
- match_mass: float32 [32768], P(('groups', 'strip')), parts along dimension 0
The draws below stay inside these ranges and needn't reach their ends.
There are 2 independent parts, one for each index of `groups`. The reference program is written for one: setup_inputs(seed, part) draws one part's arguments, and reference() takes and returns one part's arrays. A program takes and returns all parts, laid end to end along the dimension named above; each array names one. Nothing has to cross between parts.
Inputs may be any that keep to these rules, and one draw needn't show every extreme that they name: `seed_target`: values of 4096 or more mean that the point has no tie point. `edges`: the strip that an edge names exists, and its slot is below that strip's count; for a live source point at slot i the slot that an edge names lies within 16 of i.
All inputs are finite; a program needn't handle non-finite values.
Results may differ from the reference program's by a relative error of at most 0.0003.
Values may be sent and summed in bfloat16 or wider, within the bound.
No kernel may reach another device: no remote copies, remote signals or barrier semaphores. Data moves between devices by JAX's collectives and lax.ppermute only.
A program may use at most 128 MiB of HBM per device.

```python
import math
import jax
import jax.numpy as jnp
from jax import lax

FEAT = 128
POINTS_DEV = 4096
NEIGHBOURS = 8
REACH = 16
SWEEPS = 4
CAND = 4096
POINTS = 16384
TARGETS = 16384
N_STRIP = 4


def draw_src_feat(key, part):
    base = jnp.clip(jax.random.normal(jax.random.fold_in(key, 1), (FEAT, N_STRIP, POINTS_DEV), jnp.float32), -4.0, 4.0)
    return base.reshape(FEAT, POINTS).astype(jnp.bfloat16)


def draw_tgt_feat(key, part):
    base = jnp.clip(jax.random.normal(jax.random.fold_in(key, 2), (FEAT, N_STRIP, CAND), jnp.float32), -4.0, 4.0)
    return base.reshape(FEAT, TARGETS).astype(jnp.bfloat16)


def strip_layout(key):
    lowest = max(1, POINTS_DEV // 8)
    base = jax.random.randint(jax.random.fold_in(key, 21), (N_STRIP,), lowest, POINTS_DEV + 1, dtype=jnp.int32)
    fullest = jax.random.randint(jax.random.fold_in(key, 22), (), 1, N_STRIP, dtype=jnp.int32)
    step_away = jax.random.randint(jax.random.fold_in(key, 23), (), 1, N_STRIP, dtype=jnp.int32)
    lightest = (fullest + step_away) % N_STRIP
    base = base.at[fullest].set(POINTS_DEV)
    base = base.at[lightest].set(lowest)
    return (base, fullest)


def draw_counts(key, part):
    layout, fullest = strip_layout(key)
    return layout


def draw_edges(key, part):
    layout, fullest = strip_layout(key)
    shape = (NEIGHBOURS, N_STRIP, POINTS_DEV)
    strip_ids = jnp.arange(N_STRIP, dtype=jnp.int32)[None, :, None]
    slot_ids = jnp.arange(POINTS_DEV, dtype=jnp.int32)[None, None, :]
    pick = jax.random.randint(jax.random.fold_in(key, 24), shape, 0, 4, dtype=jnp.int32)
    segment = pick - (pick >= 2).astype(jnp.int32)
    target_strip = strip_ids + segment - 1
    outside = (target_strip < 0) | (target_strip >= N_STRIP)
    segment = jnp.where(outside, 1, segment)
    target_strip = strip_ids + segment - 1
    room = jnp.take(layout, target_strip)
    own = jnp.take(layout, strip_ids)
    delta = jax.random.randint(jax.random.fold_in(key, 26), shape, -REACH, REACH + 1, dtype=jnp.int32)
    wanted = slot_ids + delta
    inside = (wanted >= 0) & (wanted < room)
    fallback = jnp.clip(wanted, 0, own - 1)
    raw = jax.random.randint(jax.random.fold_in(key, 25), shape, 0, 1 << 20, dtype=jnp.int32)
    live_source = slot_ids < own
    slot = jnp.where(live_source, jnp.where(inside, wanted, fallback), raw % room)
    segment = jnp.where(live_source & jnp.logical_not(inside), 1, segment)
    values = segment * POINTS_DEV + slot
    values = values.at[0, 1, 0].set(0)
    values = values.at[1, fullest - 1, POINTS_DEV - 1].set(3 * POINTS_DEV - 1)
    return values.reshape(NEIGHBOURS, POINTS).astype(jnp.int32)


def plant(values, key, smallest, top_value):
    longest = values.shape.index(max(values.shape))
    spots = []
    for shift in (0, 1):
        where = [jax.random.randint(jax.random.fold_in(key, axis), (), 0, length) for axis, length in enumerate(values.shape)]
        where[longest] = (where[longest] + shift) % values.shape[longest]
        spots.append(tuple(where))
    return values.at[spots[0]].set(smallest).at[spots[1]].set(top_value)


def level_of(key, extent, shards, least, largest):
    def one(axis_at, parts):
        heights = jax.random.uniform(jax.random.fold_in(jax.random.fold_in(key, 6), axis_at), (parts,), jnp.float32, least / len(shards), largest / len(shards))
        return jnp.repeat(jnp.exp(heights), extent[axis_at] // parts).reshape((-1,) + (1,) * (len(extent) - axis_at - 1))

    factor_of = one(*shards[0])
    for cut in shards[1:]:
        factor_of = factor_of * one(*cut)
    return factor_of


def centred(key, shape, deviation, limit, pieces=(), kind=jnp.bfloat16):
    loudness = level_of(key, shape, pieces, -0.22, 0.18) if pieces else 1.0
    result = jax.random.normal(key, shape, jnp.float32) * deviation * loudness
    return jnp.minimum(jnp.maximum(result, -limit), limit).astype(kind)


def setup_inputs(seed: int = 0, part: int = 0) -> dict:
    key_list = jax.random.split(jax.random.key(seed), 10)
    part_keys = jax.random.split(jax.random.fold_in(key_list[9], part), 10)
    src_pos = jnp.clip(jax.random.uniform(part_keys[0], (3, POINTS), jnp.float32, -1.0, 1.0) * level_of(part_keys[0], (3, POINTS), ((1, 4),), -0.4, 0.0), -1.0, 1.0)
    src_feat = draw_src_feat(jax.random.fold_in(jax.random.fold_in(key_list[9], part), 71), part)
    tgt_pos = jnp.clip(-0.6 + 2.0 * jax.random.uniform(part_keys[2], (3, TARGETS), jnp.float32) ** level_of(part_keys[2], (3, TARGETS), ((1, 8),), -0.2, 0.2), -0.6, 1.4)
    tgt_feat = draw_tgt_feat(jax.random.fold_in(jax.random.fold_in(key_list[9], part), 71), part)
    displacement = centred(part_keys[4], (3, POINTS), 0.2, 1.0, ((1, 4),), jnp.float32)
    sigma_sq = jnp.clip(jnp.exp(math.log(2.0) - 1.3862944 * jax.random.uniform(part_keys[5], (N_STRIP,), jnp.float32) ** level_of(part_keys[5], (N_STRIP,), ((0, 4),), -0.2, 0.2)), 0.5, 2.0)
    seed_target = plant(jax.random.randint(part_keys[6], (POINTS,), 0, 2 * CAND), jax.random.fold_in(part_keys[6], 1), 0, (2 * CAND) - 1).astype(jnp.int32)
    counts = draw_counts(jax.random.fold_in(jax.random.fold_in(key_list[9], part), 71), part)
    edges = draw_edges(jax.random.fold_in(jax.random.fold_in(key_list[9], part), 71), part)
    return {"src_pos": src_pos, "src_feat": src_feat, "tgt_pos": tgt_pos, "tgt_feat": tgt_feat, "displacement": displacement, "sigma_sq": sigma_sq, "seed_target": seed_target, "counts": counts, "edges": edges}


feature_scale = 0.18
tie_gain = 3.0
outlier_level = 1.0
strip_offset = 2.0
kernel_scale = 8.0
coherence = 0.1


def strip_posterior(items):
    z_strip, feat_strip, x_strip, tfeat_strip, sigma, seeds = items
    width = min(512, POINTS_DEV)
    count = POINTS_DEV // width
    tfloat = tfeat_strip.astype(jnp.float32)
    columns = jnp.arange(CAND, dtype=jnp.int32)

    def one_block(index):
        begin = (index * width).astype(jnp.int32)
        zblock = lax.dynamic_slice_in_dim(z_strip, begin, width, 1)
        fblock = lax.dynamic_slice_in_dim(feat_strip, begin, width, 1).astype(jnp.float32)
        sblock = lax.dynamic_slice_in_dim(seeds, begin, width, 0)
        product = jnp.dot(fblock.T, tfloat, precision=lax.Precision.HIGHEST)
        dist = (x_strip[0][None, :] - zblock[0][:, None]) ** 2
        dist = dist + (x_strip[1][None, :] - zblock[1][:, None]) ** 2
        dist = dist + (x_strip[2][None, :] - zblock[2][:, None]) ** 2
        match = (columns[None, :] == sblock[:, None]).astype(jnp.float32)
        score = feature_scale * product - dist / (2.0 * sigma) + tie_gain * match
        peak = jnp.maximum(jnp.max(score, axis=1), outlier_level)
        expo = jnp.exp(score - peak[:, None])
        total = jnp.sum(expo, axis=1)
        moment = jnp.dot(x_strip, expo.T, precision=lax.Precision.HIGHEST)
        denom = total + jnp.exp(outlier_level - peak)
        return total / denom, moment / denom[None, :]

    mass, moment = lax.map(one_block, jnp.arange(count, dtype=jnp.int32))
    mass = mass.reshape(POINTS_DEV)
    moment = jnp.transpose(moment, (1, 0, 2)).reshape(3, POINTS_DEV)
    return mass, moment


def reference(src_pos, src_feat, tgt_pos, tgt_feat, displacement, sigma_sq, seed_target, counts, edges):
    strips = N_STRIP
    zpos = src_pos + displacement
    zs = jnp.transpose(zpos.reshape(3, strips, POINTS_DEV), (1, 0, 2))
    ys = jnp.transpose(src_pos.reshape(3, strips, POINTS_DEV), (1, 0, 2))
    vs = jnp.transpose(displacement.reshape(3, strips, POINTS_DEV), (1, 0, 2))
    fs = jnp.transpose(src_feat.reshape(FEAT, strips, POINTS_DEV), (1, 0, 2))
    xs = jnp.transpose(tgt_pos.reshape(3, strips, CAND), (1, 0, 2))
    txs = jnp.transpose(tgt_feat.reshape(FEAT, strips, CAND), (1, 0, 2))
    seeds = seed_target.reshape(strips, POINTS_DEV)
    mass, moment = lax.map(strip_posterior, (zs, fs, xs, txs, sigma_sq, seeds))
    slots = jnp.arange(POINTS_DEV, dtype=jnp.int32)
    live = (slots[None, :] < counts[:, None]).astype(jnp.float32)
    mass = mass * live
    moment = moment * live[:, None, :]
    resid = moment - mass[:, None, :] * zs
    geometry = jnp.concatenate([ys, live[:, None, :]], axis=1)
    padded = jnp.pad(geometry, ((1, 1), (0, 0), (0, 0)))
    flat_geo = jnp.transpose(padded, (1, 0, 2)).reshape(4, (strips + 2) * POINTS_DEV)
    edge = jnp.transpose(edges.reshape(NEIGHBOURS, strips, POINTS_DEV), (1, 0, 2))
    segment = edge // POINTS_DEV
    local = edge % POINTS_DEV
    strip_ids = jnp.arange(strips, dtype=jnp.int32)
    flat = ((strip_ids[:, None, None] + segment) * POINTS_DEV + local).astype(jnp.int32)
    neigh = flat_geo[:, flat]
    shift = strip_offset * (segment - 1).astype(jnp.float32)
    d0 = ys[:, 0][:, None, :] - neigh[0] - shift
    d1 = ys[:, 1][:, None, :] - neigh[1]
    d2 = ys[:, 2][:, None, :] - neigh[2]
    kernel = live[:, None, :] * neigh[3] * jnp.exp(-(d0 * d0 + d1 * d1 + d2 * d2) / (2.0 * kernel_scale)) / NEIGHBOURS

    def spread(field):
        fpad = jnp.pad(field, ((1, 1), (0, 0), (0, 0)))
        fflat = jnp.transpose(fpad, (1, 0, 2)).reshape(3, (strips + 2) * POINTS_DEV)
        got = fflat[:, flat]
        return jnp.transpose(jnp.sum(kernel[None] * got, axis=2), (1, 0, 2))

    diag = mass + coherence * sigma_sq[:, None]
    field = resid / diag[:, None, :]
    for sweep in range(SWEEPS):
        field = (resid - mass[:, None, :] * spread(field)) / diag[:, None, :]
    new_disp = vs + field + spread(field)
    new_disp = jnp.transpose(new_disp, (1, 0, 2)).reshape(3, POINTS)
    return new_disp, mass.reshape(POINTS)
```

```python
import functools

import jax
import jax.numpy as jnp
from jax import lax
from jax.experimental import pallas as pl
from jax.experimental.pallas import tpu as pltpu
from jax.sharding import PartitionSpec as P

REACH = 16
SWEEPS = 4
EDGES = 8
SPAN = 2 * REACH + 1
LANES = 128
ROWS_WIN = 24
KEEP = LANES - 2 * REACH

feature_scale = 0.18
tie_gain = 3.0
outlier_level = 1.0
strip_offset = 2.0
kernel_scale = 8.0
coherence = 0.1

LOG2E = 1.4426950408889634
VMEM = pl.BlockSpec(memory_space=pltpu.VMEM)
SMEM = pl.BlockSpec(memory_space=pltpu.SMEM)
F32 = jnp.float32
BF16 = jnp.bfloat16


def three_parts(value):
    first = value.astype(BF16).astype(F32)
    rest = value - first
    second = rest.astype(BF16).astype(F32)
    third = (rest - second).astype(BF16).astype(F32)
    return first, second, third


def lane_ids(rows=1):
    return lax.broadcasted_iota(jnp.int32, (rows, LANES), 1)


def prepare_kernel(
    ints, floats, src_pos, disp, tgt_pos, seeds, edges, geo, z_out, disp_out, cols, aug, x_cols, rows
):
    base = ints[0]
    offset = ints[1]
    slots = src_pos.shape[1]
    sigma = floats[0]
    blocks = cols.shape[0] // LANES
    cands = tgt_pos.shape[1]
    scale = 1.0 / (sigma * feature_scale)
    rows[...] = jnp.zeros_like(rows)
    for at in range(blocks):
        here = pl.ds(pl.multiple_of(base + at * LANES, LANES), LANES)
        pos = src_pos[:, here]
        move = disp[:, here]
        z = pos + move
        edge = edges[:, here]
        slot = base + at * LANES + lane_ids()
        segment = edge // slots
        local = edge - segment * slots
        away = jnp.clip(local - slot + REACH, 0, SPAN - 1)
        code = (segment * SPAN + away).astype(F32)
        high = pos.astype(BF16).astype(F32)
        low = pos - high
        for k in range(EDGES):
            rows[k * blocks + at : k * blocks + at + 1, :] = code[k : k + 1, :]
        for c in range(3):
            put = (EDGES + c) * blocks + at
            rows[put : put + 1, :] = high[c : c + 1, :]
            put = (EDGES + 3 + c) * blocks + at
            rows[put : put + 1, :] = low[c : c + 1, :]
            z_out[c, at : at + 1, :] = z[c : c + 1, :]
            disp_out[c, at : at + 1, :] = move[c : c + 1, :]
        first, second, third = three_parts(z * scale)
        norm = jnp.sum(z * z, axis=0, keepdims=True) * (0.5 / sigma)
        level = (norm + outlier_level) * LOG2E
        seed = (seeds[:, here] - offset).astype(F32)
        ones = jnp.ones((3, LANES), F32)
        tile = jnp.concatenate(
            [first, first, second, second, first, third, ones, seed, level]
            + [jnp.zeros((9, LANES), F32)],
            axis=0,
        )
        cols[at * LANES : (at + 1) * LANES, :] = jnp.concatenate(
            [tile.T, jnp.zeros((LANES, LANES - 32), F32)], axis=1
        )
    geo[...] = rows[...].astype(BF16)
    for at in range(cands // LANES):
        here = pl.ds(at * LANES, LANES)
        x = tgt_pos[:, here]
        first, second, third = three_parts(x)
        norm = jnp.sum(x * x, axis=0, keepdims=True) * (-0.5 * scale)
        parts = three_parts(norm)
        aug[:, here] = jnp.concatenate(
            [first, second, first, second, third, first, *parts, jnp.zeros((LANES - 21, LANES), F32)],
            axis=0,
        ).astype(BF16)
        one = jnp.ones((1, LANES), F32)
        gap = jnp.zeros((5, LANES), F32)
        tile = jnp.concatenate(
            [first, one, gap[:4], second, gap, third, gap, jnp.zeros((8, LANES), F32)], axis=0
        )
        x_cols[at * LANES : (at + 1) * LANES, :] = jnp.concatenate(
            [tile.T, jnp.zeros((LANES, LANES - 32), F32)], axis=1
        ).astype(BF16)


def score_kernel(
    ints, src_own, src_other, tgt_own, tgt_other, cols, aug, x_cols, state, left, score, highest, *, chunk, tile
):
    base = ints[0]
    points = cols.shape[0]
    blocks = points // LANES
    cands = aug.shape[1]
    half = src_own.shape[0]
    for at in range(blocks):
        here = pl.ds(pl.multiple_of(base + at * LANES, LANES), LANES)
        down = slice(at * LANES, (at + 1) * LANES)
        both = jnp.concatenate([src_own[:, here], src_other[:, here]], axis=0)
        left[down, 0 : 2 * half] = both.T
        left[down, 2 * half :] = cols[down, :].astype(BF16)
    tiles = cands // tile
    per = tile // LANES
    for t in range(tiles):
        across = slice(t * tile, (t + 1) * tile)
        right = jnp.concatenate([tgt_own[:, across], tgt_other[:, across], aug[:, across]], axis=0)
        for r in range(0, points, chunk):
            product = jnp.dot(left[r : r + chunk, :], right, preferred_element_type=F32)
            score[t, r : r + chunk] = product
            top = product[:, :LANES]
            for q in range(1, per):
                top = jnp.maximum(top, product[:, q * LANES : (q + 1) * LANES])
            highest[r : r + chunk] = top if t == 0 else jnp.maximum(highest[r : r + chunk], top)
    ids = lax.broadcasted_iota(jnp.int32, (1, tile), 1).astype(F32)
    state[...] = jnp.zeros_like(state)
    for r in range(0, points, chunk):
        seed = cols[r : r + chunk, 21:22]
        level = cols[r : r + chunk, 22:23]
        top = jnp.max(highest[r : r + chunk], axis=1, keepdims=True) * (feature_scale * LOG2E)
        peak = jnp.maximum(top, level)
        tied = peak - tie_gain * LOG2E
        total = jnp.zeros((chunk, LANES), F32)
        for t in range(tiles):
            shift = jnp.where(ids + float(t * tile) == seed, tied, peak)
            weight = jnp.exp2(score[t, r : r + chunk] * (feature_scale * LOG2E) - shift)
            high = weight.astype(BF16)
            low = (weight - high.astype(F32)).astype(BF16)
            x = x_cols[t * tile : (t + 1) * tile, :]
            total += jnp.dot(high, x, preferred_element_type=F32)
            total += jnp.dot(low, x, preferred_element_type=F32)
        total = jnp.where(lane_ids() == 4, peak, total)
        highest[r : r + chunk] = total
    for at in range(blocks):
        flat = highest[at * LANES : (at + 1) * LANES, :].T
        summed = flat[0:8] + flat[8:16] + flat[16:24]
        for q in range(5):
            state[q * blocks + at : q * blocks + at + 1, :] = summed[q : q + 1, :]


def merge_kernel(ints, floats, z_ref, *refs):
    *states, terms, mass_out = refs
    blocks = z_ref.shape[1]
    sigma = floats[0]

    def part(ref, q):
        return ref[q * blocks : (q + 1) * blocks, :]

    peak = part(states[0], 4)
    for ref in states[1:]:
        peak = jnp.maximum(peak, part(ref, 4))
    sums = [jnp.zeros((blocks, LANES), F32)] * 4
    for ref in states:
        factor = jnp.exp2(part(ref, 4) - peak)
        sums = [s + part(ref, q) * factor for q, s in enumerate(sums)]
    z = [z_ref[c] for c in range(3)]
    norm = (z[0] * z[0] + z[1] * z[1] + z[2] * z[2]) * (0.5 / sigma)
    slot = ints[0] + LANES * lax.broadcasted_iota(jnp.int32, (blocks, LANES), 0) + lane_ids(blocks)
    live = (slot < ints[2]).astype(F32)
    denom = sums[3] + jnp.exp2((norm + outlier_level) * LOG2E - peak)
    each = live / denom
    mass = sums[3] * each
    diag = mass + coherence * sigma
    inverse = 1.0 / diag
    terms[...] = jnp.zeros_like(terms)
    for c in range(3):
        terms[c * blocks : (c + 1) * blocks, :] = (sums[c] * each - mass * z[c]) * inverse
    terms[3 * blocks : 4 * blocks, :] = mass * inverse
    mass_out[...] = mass


def to_windows(rows, put):
    lane = lane_ids()
    groups = ROWS_WIN // 4
    for w, begin in enumerate((-REACH, KEEP - REACH, 2 * KEEP - REACH, 3 * KEEP - REACH)):
        row = begin // LANES
        start = begin - row * LANES
        first = rows[pl.ds(8 + row, groups, stride=3), :]
        second = rows[pl.ds(9 + row, groups, stride=3), :]
        put(w, pltpu.roll(jnp.where(lane >= start, first, second), LANES - start, 1))


def fill_rows(rows, values):
    blocks = values.shape[0]
    rows[8 : 8 + blocks, :] = values


def pick(value, index):
    return jnp.take_along_axis(value, index, axis=1, mode="promise_in_bounds")


def each_strip(count, body):
    if count <= 4:
        for j in range(count):
            body(j)
    else:
        lax.fori_loop(0, count, lambda j, c: (body(j), c)[1], 0)


def kernels_kernel(ints, *refs, strips, blocks):
    geos = refs[:strips]
    index_out, segment_out, weight_out, wide, rows, codes, places = refs[strips:]
    me = ints[3]
    groups = ROWS_WIN // 4
    lane = lane_ids(8)
    rows[...] = jnp.zeros_like(rows)
    places[0] = jnp.zeros_like(places[0])
    places[strips + 1] = jnp.zeros_like(places[0])

    for d in range(strips):
        wide[...] = geos[d][...].astype(F32)
        j = lax.rem(me + d, strips)

        for k in range(EDGES):
            fill_rows(rows, wide[k * blocks : (k + 1) * blocks, :])

            def put_code(w, value, k=k, j=j):
                codes[j, k, pl.ds(w, groups, stride=4), :] = value

            to_windows(rows, put_code)
        for c in range(3):
            at = (EDGES + c) * blocks
            more = at + 3 * blocks
            fill_rows(rows, wide[at : at + blocks, :] + wide[more : more + blocks, :])

            def put_place(w, value, c=c, j=j):
                places[j + 1, c, pl.ds(w, groups, stride=4), :] = value

            to_windows(rows, put_place)

    def one_strip(j):
        for v in range(ROWS_WIN // 8):
            down = slice(8 * v, 8 * v + 8)
            own = [places[j + 1, c, down, :] for c in range(3)]
            near = [[places[j + g, c, down, :] for c in range(3)] for g in range(3)]
            for k in range(EDGES):
                code = codes[j, k, down, :].astype(jnp.int32)
                later = code >= SPAN
                last = code >= 2 * SPAN
                segment = later.astype(jnp.int32) + last.astype(jnp.int32)
                index = jnp.clip(lane + code - segment * SPAN - REACH, 0, LANES - 1)
                total = None
                for c in range(3):
                    got = jnp.where(
                        last,
                        pick(near[2][c], index),
                        jnp.where(later, pick(near[1][c], index), pick(near[0][c], index)),
                    )
                    gap = own[c] - got
                    if c == 0:
                        gap = gap - strip_offset * (segment - 1).astype(F32)
                    total = gap * gap if total is None else total + gap * gap
                weight_out[j, k, down, :] = jnp.exp(total * (-0.5 / kernel_scale)) * (1.0 / EDGES)
                index_out[j, k, down, :] = index
                segment_out[j, k, down, :] = segment

    each_strip(strips, one_strip)


def sweep_kernel(ints, *refs, strips, blocks):
    terms = refs[:strips]
    index, segment, weight, disp, mass, out = refs[strips : strips + 6]
    rows, base, gain, even, odd, last_rows = refs[strips + 6 :]
    me = ints[3]
    core = ints[4]
    groups = ROWS_WIN // 4
    parts = ROWS_WIN // 8
    lane = lane_ids(8)
    rows[...] = jnp.zeros_like(rows)
    for field in (even, odd):
        field[...] = jnp.zeros_like(field)

    for d in range(strips):
        j = lax.rem(me + d, strips)
        for q in range(4):
            fill_rows(rows, terms[d][q * blocks : (q + 1) * blocks, :])

            def put(w, value, q=q, j=j):
                if q < 3:
                    base[j, q, pl.ds(w, groups, stride=4), :] = value
                    even[j + 1, q, pl.ds(8 + w, groups, stride=4), :] = value
                else:
                    gain[j, pl.ds(w, groups, stride=4), :] = value

            to_windows(rows, put)

    def spread(field, j, v):
        down = slice(8 * v, 8 * v + 8)
        inner = slice(8 * v + 8, 8 * v + 16)
        near = [[field[j + g, c, inner, :] for c in range(3)] for g in range(3)]
        sums = [None] * 3
        for k in range(EDGES):
            at = index[j, k, down, :]
            part = segment[j, k, down, :]
            later = part >= 1
            last = part >= 2
            size = weight[j, k, down, :]
            for c in range(3):
                got = jnp.where(
                    last,
                    pick(near[2][c], at),
                    jnp.where(later, pick(near[1][c], at), pick(near[0][c], at)),
                )
                sums[c] = size * got if sums[c] is None else sums[c] + size * got
        return sums

    for sweep in range(SWEEPS):
        now, after = (even, odd) if sweep % 2 == 0 else (odd, even)
        wanted = SWEEPS - sweep

        def one_strip(j, now=now, after=after, wanted=wanted):
            @pl.when(jnp.abs(me - j) <= wanted)
            def _():
                for v in range(parts):
                    down = slice(8 * v, 8 * v + 8)
                    inner = slice(8 * v + 8, 8 * v + 16)
                    sums = spread(now, j, v)
                    for c in range(3):
                        after[j + 1, c, inner, :] = base[j, c, down, :] - gain[j, down, :] * sums[c]
                for c in range(3):
                    for v in range(parts):
                        at = 8 * v + 8
                        here = after[j + 1, c, at : at + 8, :]
                        before = after[j + 1, c, at - 1 : at + 7, :]
                        behind = after[j + 1, c, at + 1 : at + 9, :]
                        after[j + 1, c, at : at + 8, :] = jnp.where(
                            lane < REACH,
                            pltpu.roll(before, 2 * REACH, 1),
                            jnp.where(lane >= LANES - REACH, pltpu.roll(behind, KEEP, 1), here),
                        )

        each_strip(strips, one_strip)

    field = even if SWEEPS % 2 == 0 else odd
    for v in range(parts):
        sums = spread(field, me, v)
        for c in range(3):
            last_rows[c, 8 * v : 8 * v + 8, :] = sums[c] + field[me + 1, c, 8 * v + 8 : 8 * v + 16, :]
    wide_lane = lane_ids()
    many = ROWS_WIN // 4
    for c in range(3):
        for i in range(3):
            begin = LANES * i - KEEP * i + REACH
            first = last_rows[c, pl.ds(i, many, stride=4), :]
            second = last_rows[c, pl.ds(i + 1, many, stride=4), :]
            held = KEEP - (LANES - KEEP) * i
            value = jnp.where(
                wide_lane < held,
                pltpu.roll(first, LANES - begin, 1),
                pltpu.roll(second, (held - REACH) % LANES, 1),
            )
            rows[pl.ds(i, many, stride=3), :] = value
        slot = ints[0] + LANES * lax.broadcasted_iota(jnp.int32, (blocks, LANES), 0) + lane_ids(blocks)
        rows[0:blocks, :] = disp[c] + jnp.where(slot < ints[2], rows[0:blocks, :], 0.0)
        for at in range(blocks - 1):
            out[c : c + 1, at * LANES : (at + 1) * LANES] = rows[pl.ds(core + at, 1), :]
    rows[0:blocks, :] = mass[...]
    for at in range(blocks - 1):
        out[3:4, at * LANES : (at + 1) * LANES] = rows[pl.ds(core + at, 1), :]


def around(array, axis):
    count = lax.axis_size(axis)
    return [array] + [
        lax.ppermute(array, axis, [((i + d) % count, i) for i in range(count)]) for d in range(1, count)
    ]


def on_device(
    src_pos, src_feat, tgt_pos, tgt_feat, displacement, sigma_sq, seed_target, counts, edges
):
    slots = src_pos.shape[1]
    cands = tgt_pos.shape[1]
    strips = lax.axis_size("strip")
    half = slots // 2
    points = half + LANES
    blocks = points // LANES
    core = lax.axis_index("feat")
    base = core * (half - LANES)
    ints = jnp.stack(
        [base, lax.axis_index("cand") * cands, counts[0], lax.axis_index("strip"), core]
    ).astype(jnp.int32)

    src_other = around(src_feat, "feat")[1]
    tgt_other = around(tgt_feat, "feat")[1]

    geo_rows = 16 * ((14 * blocks + 15) // 16)
    geo, z, disp, cols, aug, x_cols = pl.pallas_call(
        prepare_kernel,
        name="prepare",
        out_shape=(
            jax.ShapeDtypeStruct((geo_rows, LANES), BF16),
            jax.ShapeDtypeStruct((3, blocks, LANES), F32),
            jax.ShapeDtypeStruct((3, blocks, LANES), F32),
            jax.ShapeDtypeStruct((points, LANES), F32),
            jax.ShapeDtypeStruct((LANES, cands), BF16),
            jax.ShapeDtypeStruct((cands, LANES), BF16),
        ),
        in_specs=[SMEM, SMEM] + [VMEM] * 5,
        out_specs=(VMEM,) * 6,
        scratch_shapes=[pltpu.VMEM((geo_rows, LANES), F32)],
    )(ints, sigma_sq, src_pos, displacement, tgt_pos, seed_target.reshape(1, slots), edges)

    geos = around(geo, "strip")

    chunk = points // 8
    tile = 256
    state_rows = 8 * ((5 * blocks + 7) // 8)
    state = pl.pallas_call(
        functools.partial(score_kernel, chunk=chunk, tile=tile),
        name="score",
        out_shape=jax.ShapeDtypeStruct((state_rows, LANES), F32),
        in_specs=[SMEM] + [VMEM] * 7,
        out_specs=VMEM,
        scratch_shapes=[
            pltpu.VMEM((points, 2 * LANES), BF16),
            pltpu.VMEM((cands // tile, points, tile), F32),
            pltpu.VMEM((points, LANES), F32),
        ],
        compiler_params=pltpu.CompilerParams(vmem_limit_bytes=48 << 20),
    )(ints, src_feat, src_other, tgt_feat, tgt_other, cols, aug, x_cols)

    states = around(state, "cand")
    term_rows = 8 * ((4 * blocks + 7) // 8)
    terms, mass = pl.pallas_call(
        merge_kernel,
        name="merge",
        out_shape=(
            jax.ShapeDtypeStruct((term_rows, LANES), F32),
            jax.ShapeDtypeStruct((blocks, LANES), F32),
        ),
        in_specs=[SMEM, SMEM] + [VMEM] * (1 + len(states)),
        out_specs=(VMEM, VMEM),
    )(ints, sigma_sq, z, *states)

    all_terms = around(terms, "strip")

    shape = (strips, EDGES, ROWS_WIN, LANES)
    index, segment, weight = pl.pallas_call(
        functools.partial(kernels_kernel, strips=strips, blocks=blocks),
        name="neighbours",
        out_shape=(
            jax.ShapeDtypeStruct(shape, jnp.int32),
            jax.ShapeDtypeStruct(shape, jnp.int32),
            jax.ShapeDtypeStruct(shape, F32),
        ),
        in_specs=[SMEM] + [VMEM] * strips,
        out_specs=(VMEM,) * 3,
        scratch_shapes=[
            pltpu.VMEM((geo_rows, LANES), F32),
            pltpu.VMEM((ROWS_WIN + 16, LANES), F32),
            pltpu.VMEM(shape, F32),
            pltpu.VMEM((strips + 2, 3, ROWS_WIN, LANES), F32),
        ],
    )(ints, *geos)

    field_shape = (strips + 2, 3, ROWS_WIN + 16, LANES)
    part = pl.pallas_call(
        functools.partial(sweep_kernel, strips=strips, blocks=blocks),
        name="sweeps",
        out_shape=jax.ShapeDtypeStruct((4, half), F32),
        in_specs=[SMEM] + [VMEM] * (strips + 5),
        out_specs=VMEM,
        scratch_shapes=[
            pltpu.VMEM((ROWS_WIN + 16, LANES), F32),
            pltpu.VMEM((strips, 3, ROWS_WIN, LANES), F32),
            pltpu.VMEM((strips, ROWS_WIN, LANES), F32),
            pltpu.VMEM(field_shape, F32),
            pltpu.VMEM(field_shape, F32),
            pltpu.VMEM((3, ROWS_WIN + 8, LANES), F32),
        ],
    )(ints, *all_terms, index, segment, weight, disp, mass)

    whole = lax.all_gather(part, "feat", axis=1, tiled=True)
    return (whole[0:3], whole[3])


def solution(mesh):
    in_specs = (
        P(None, ("groups", "strip")),
        P("feat", ("groups", "strip")),
        P(None, ("groups", "strip", "cand")),
        P("feat", ("groups", "strip", "cand")),
        P(None, ("groups", "strip")),
        P(("groups", "strip")),
        P(("groups", "strip")),
        P(("groups", "strip")),
        P(None, ("groups", "strip")),
    )
    out_specs = (P(None, ("groups", "strip")), P(("groups", "strip")))
    return jax.shard_map(
        on_device, mesh=mesh, in_specs=in_specs, out_specs=out_specs, check_vma=False
    )
```

```python
import functools

import jax
import jax.numpy as jnp
from jax import lax
from jax.experimental import pallas as pl
from jax.experimental.pallas import tpu as pltpu
from jax.sharding import PartitionSpec as P

REACH = 16
SWEEPS = 4
EDGES = 8
SPAN = 2 * REACH + 1
LANES = 128
ROWS_WIN = 24
KEEP = LANES - 2 * REACH

feature_scale = 0.18
tie_gain = 3.0
outlier_level = 1.0
strip_offset = 2.0
kernel_scale = 8.0
coherence = 0.1

LOG2E = 1.4426950408889634
VMEM = pl.BlockSpec(memory_space=pltpu.VMEM)
F32 = jnp.float32
BF16 = jnp.bfloat16


def first_slot(slots):
    return lax.axis_index("feat") * (slots // 2 - LANES)


def three_parts(value):
    first = value.astype(BF16).astype(F32)
    rest = value - first
    second = rest.astype(BF16).astype(F32)
    third = (rest - second).astype(BF16).astype(F32)
    return first, second, third


def lane_ids(rows=1):
    return lax.broadcasted_iota(jnp.int32, (rows, LANES), 1)


def copies_in(sources, targets, done):
    copies = [
        pltpu.make_async_copy(source, target, done.at[n])
        for n, (source, target) in enumerate(zip(sources, targets))
    ]
    for copy in copies:
        copy.start()
    return copies


def geometry_kernel(
    far_pos, far_disp, far_edges, far_counts, far_sigma, geo, z_out, disp_out, src_pos, disp, edges, counts, sigma, rows, done
):
    slots = src_pos.shape[1]
    base = first_slot(slots)
    blocks = z_out.shape[1]
    copies = copies_in(
        [far_pos, far_disp, far_edges, far_counts, far_sigma], [src_pos, disp, edges, counts, sigma], done
    )
    rows[...] = jnp.zeros_like(rows)
    for copy in copies:
        copy.wait()
    for at in range(blocks):
        here = pl.ds(pl.multiple_of(base + at * LANES, LANES), LANES)
        pos = src_pos[:, here]
        move = disp[:, here]
        z = pos + move
        edge = edges[:, here]
        slot = base + at * LANES + lane_ids()
        segment = edge // slots
        local = edge - segment * slots
        away = jnp.clip(local - slot + REACH, 0, SPAN - 1)
        code = (segment * SPAN + away).astype(F32)
        high = pos.astype(BF16).astype(F32)
        low = pos - high
        for k in range(EDGES):
            rows[k * blocks + at : k * blocks + at + 1, :] = code[k : k + 1, :]
        for c in range(3):
            put = (EDGES + c) * blocks + at
            rows[put : put + 1, :] = high[c : c + 1, :]
            put = (EDGES + 3 + c) * blocks + at
            rows[put : put + 1, :] = low[c : c + 1, :]
            z_out[c, at : at + 1, :] = z[c : c + 1, :]
            disp_out[c, at : at + 1, :] = move[c : c + 1, :]
    live = (slot_ids(slots, blocks) < counts[0]).astype(F32)
    z_out[3] = live
    z_out[4] = jnp.full((blocks, LANES), sigma[0], F32)
    disp_out[3] = live
    geo[...] = rows[...].astype(BF16)


def score_kernel(*refs, chunk, tile):
    far, state, near = refs[:9], refs[9], refs[10:19]
    cols, aug, x_cols, left, score, highest, done = refs[19:]
    slots = far[1].shape[1]
    points = cols.shape[0]
    mine = pl.ds(pl.multiple_of(first_slot(slots), LANES), points)
    sources = [*far[:5], far[5].at[:, mine], far[6].at[:, mine], far[7], far[8]]
    copies = copies_in(sources, near, done)
    for copy in copies[:5]:
        copy.wait()
    prepare(*near[:5], cols, aug, x_cols)
    for copy in copies[5:]:
        copy.wait()
    score_all(*near[5:], cols, aug, x_cols, state, left, score, highest, chunk=chunk, tile=tile)


def prepare(sigmas, src_pos, disp, tgt_pos, seeds, cols, aug, x_cols):
    slots = src_pos.shape[1]
    base = first_slot(slots)
    sigma = sigmas[0]
    blocks = cols.shape[0] // LANES
    cands = tgt_pos.shape[1]
    offset = lax.axis_index("cand") * cands
    scale = 1.0 / (sigma * feature_scale)
    for at in range(blocks):
        here = pl.ds(pl.multiple_of(base + at * LANES, LANES), LANES)
        z = src_pos[:, here] + disp[:, here]
        first, second, third = three_parts(z * scale)
        norm = jnp.sum(z * z, axis=0, keepdims=True) * (0.5 / sigma)
        level = (norm + outlier_level) * LOG2E
        seed = (seeds[:, here] - offset).astype(F32)
        ones = jnp.ones((3, LANES), F32)
        tile = jnp.concatenate(
            [first, first, second, second, first, third, ones, seed, level]
            + [jnp.zeros((9, LANES), F32)],
            axis=0,
        )
        cols[at * LANES : (at + 1) * LANES, :] = jnp.concatenate(
            [tile.T, jnp.zeros((LANES, LANES - 32), F32)], axis=1
        )
    for at in range(cands // LANES):
        here = pl.ds(at * LANES, LANES)
        x = tgt_pos[:, here]
        first, second, third = three_parts(x)
        norm = jnp.sum(x * x, axis=0, keepdims=True) * (-0.5 * scale)
        parts = three_parts(norm)
        aug[:, here] = jnp.concatenate(
            [first, second, first, second, third, first, *parts, jnp.zeros((LANES - 21, LANES), F32)],
            axis=0,
        ).astype(BF16)
        one = jnp.ones((1, LANES), F32)
        gap = jnp.zeros((5, LANES), F32)
        tile = jnp.concatenate(
            [first, one, gap[:4], second, gap, third, gap, jnp.zeros((8, LANES), F32)], axis=0
        )
        x_cols[at * LANES : (at + 1) * LANES, :] = jnp.concatenate(
            [tile.T, jnp.zeros((LANES, LANES - 32), F32)], axis=1
        ).astype(BF16)


def score_all(src_own, src_other, tgt_own, tgt_other, cols, aug, x_cols, state, left, score, highest, *, chunk, tile):
    points = cols.shape[0]
    blocks = points // LANES
    cands = aug.shape[1]
    half = src_own.shape[0]
    for at in range(blocks):
        down = slice(at * LANES, (at + 1) * LANES)
        both = jnp.concatenate([src_own[:, down], src_other[:, down]], axis=0)
        left[down, 0 : 2 * half] = both.T
        left[down, 2 * half :] = cols[down, :].astype(BF16)
    tiles = cands // tile
    per = tile // LANES
    for t in range(tiles):
        across = slice(t * tile, (t + 1) * tile)
        right = jnp.concatenate([tgt_own[:, across], tgt_other[:, across], aug[:, across]], axis=0)
        for r in range(0, points, chunk):
            product = jnp.dot(left[r : r + chunk, :], right, preferred_element_type=F32)
            score[t, r : r + chunk] = product
            top = product[:, :LANES]
            for q in range(1, per):
                top = jnp.maximum(top, product[:, q * LANES : (q + 1) * LANES])
            highest[r : r + chunk] = top if t == 0 else jnp.maximum(highest[r : r + chunk], top)
    ids = lax.broadcasted_iota(jnp.int32, (1, tile), 1).astype(F32)
    state[...] = jnp.zeros_like(state)
    for r in range(0, points, chunk):
        seed = cols[r : r + chunk, 21:22]
        level = cols[r : r + chunk, 22:23]
        top = jnp.max(highest[r : r + chunk], axis=1, keepdims=True) * (feature_scale * LOG2E)
        peak = jnp.maximum(top, level)
        tied = peak - tie_gain * LOG2E
        total = jnp.zeros((chunk, LANES), F32)
        for t in range(tiles):
            shift = jnp.where(ids + float(t * tile) == seed, tied, peak)
            weight = jnp.exp2(score[t, r : r + chunk] * (feature_scale * LOG2E) - shift)
            high = weight.astype(BF16)
            low = (weight - high.astype(F32)).astype(BF16)
            x = x_cols[t * tile : (t + 1) * tile, :]
            total += jnp.dot(high, x, preferred_element_type=F32)
            total += jnp.dot(low, x, preferred_element_type=F32)
        total = jnp.where(lane_ids() == 4, peak, total)
        highest[r : r + chunk] = total
    for at in range(blocks):
        flat = highest[at * LANES : (at + 1) * LANES, :].T
        summed = flat[0:8] + flat[8:16] + flat[16:24]
        for q in range(5):
            state[q * blocks + at : q * blocks + at + 1, :] = summed[q : q + 1, :]


def slot_ids(slots, blocks):
    rows = lax.broadcasted_iota(jnp.int32, (blocks, LANES), 0)
    return first_slot(slots) + LANES * rows + lane_ids(blocks)


def merge_kernel(z_ref, *refs):
    *states, _, terms, mass_out = refs
    blocks = z_ref.shape[1]
    live = z_ref[3]
    sigma = z_ref[4]

    def part(ref, q):
        return ref[q * blocks : (q + 1) * blocks, :]

    peak = part(states[0], 4)
    for ref in states[1:]:
        peak = jnp.maximum(peak, part(ref, 4))
    sums = [jnp.zeros((blocks, LANES), F32)] * 4
    for ref in states:
        factor = jnp.exp2(part(ref, 4) - peak)
        sums = [s + part(ref, q) * factor for q, s in enumerate(sums)]
    z = [z_ref[c] for c in range(3)]
    norm = (z[0] * z[0] + z[1] * z[1] + z[2] * z[2]) * (0.5 / sigma)
    denom = sums[3] + jnp.exp2((norm + outlier_level) * LOG2E - peak)
    each = live / denom
    mass = sums[3] * each
    diag = mass + coherence * sigma
    inverse = 1.0 / diag
    terms[...] = jnp.zeros_like(terms)
    for c in range(3):
        terms[c * blocks : (c + 1) * blocks, :] = (sums[c] * each - mass * z[c]) * inverse
    terms[3 * blocks : 4 * blocks, :] = mass * inverse
    mass_out[...] = mass


def to_windows(rows, put):
    lane = lane_ids()
    groups = ROWS_WIN // 4
    for w, begin in enumerate((-REACH, KEEP - REACH, 2 * KEEP - REACH, 3 * KEEP - REACH)):
        row = begin // LANES
        start = begin - row * LANES
        first = rows[pl.ds(8 + row, groups, stride=3), :]
        second = rows[pl.ds(9 + row, groups, stride=3), :]
        put(w, pltpu.roll(jnp.where(lane >= start, first, second), LANES - start, 1))


def fill_rows(rows, values):
    blocks = values.shape[0]
    rows[8 : 8 + blocks, :] = values


def pick(value, index):
    return jnp.take_along_axis(value, index, axis=1, mode="promise_in_bounds")


def each_strip(count, body):
    if count <= 4:
        for j in range(count):
            body(j)
    else:
        lax.fori_loop(0, count, lambda j, c: (body(j), c)[1], 0)


def packed(values):
    first, second, third = (value.astype(jnp.int32) for value in values)
    third = third + (1 << 20)
    return (first << 11) + (third >> 10), (second << 11) + (third & 1023)


def unpacked(words):
    first, second = words
    third = ((first & 2047) << 10) + (second & 1023) - (1 << 20)
    return [value.astype(F32) for value in (first >> 11, second >> 11, third)]


def picked(words, index, later, last, ends):
    low, high = ends
    got = []
    for w in range(len(words[1])):
        value = pick(words[1][w], index)
        if not low:
            value = jnp.where(later, value, pick(words[0][w], index))
        if not high:
            value = jnp.where(last, pick(words[2][w], index), value)
        got.append(value)
    return got


def ends_of(j, strips):
    return (j == 0, j == strips - 1) if isinstance(j, int) else (False, False)


def kernels_kernel(*refs, strips, blocks):
    geos = refs[:strips]
    index_out, segment_out, weight_out, wide, rows, codes, raw, places = refs[strips:]
    groups = ROWS_WIN // 4
    lane = lane_ids(8)
    rows[...] = jnp.zeros_like(rows)
    places[0] = jnp.zeros_like(places[0])
    places[strips + 1] = jnp.zeros_like(places[0])
    unit = float(1 << 19)

    for d in range(strips):
        wide[...] = geos[d][...].astype(F32)
        j = lax.rem(lax.axis_index("strip") + d, strips)

        for k in range(EDGES):
            fill_rows(rows, wide[k * blocks : (k + 1) * blocks, :])

            def put_code(w, value, k=k, j=j):
                codes[j, k, pl.ds(w, groups, stride=4), :] = value

            to_windows(rows, put_code)
        for c in range(3):
            at = (EDGES + c) * blocks
            more = at + 3 * blocks
            fill_rows(rows, wide[at : at + blocks, :] + wide[more : more + blocks, :])

            def put_place(w, value, c=c):
                raw[c, pl.ds(w, groups, stride=4), :] = value

            to_windows(rows, put_place)
        for q, word in enumerate(packed([raw[c] * unit for c in range(3)])):
            places[j + 1, q] = word

    def one_strip(j):
        ends = ends_of(j, strips)
        for v in range(ROWS_WIN // 8):
            down = slice(8 * v, 8 * v + 8)
            near = [[places[j + g, q, down, :] for q in range(2)] for g in range(3)]
            own = unpacked(near[1])
            for k in range(EDGES):
                code = codes[j, k, down, :].astype(jnp.int32)
                later = code >= SPAN
                last = code >= 2 * SPAN
                segment = later.astype(jnp.int32) + last.astype(jnp.int32)
                index = jnp.clip(lane + code - segment * SPAN - REACH, 0, LANES - 1)
                got = unpacked(picked(near, index, later, last, ends))
                gaps = [(own[c] - got[c]) * (1.0 / unit) for c in range(3)]
                gaps[0] = gaps[0] - strip_offset * (segment - 1).astype(F32)
                total = gaps[0] * gaps[0] + gaps[1] * gaps[1] + gaps[2] * gaps[2]
                weight_out[j, k, down, :] = jnp.exp(total * (-0.5 / kernel_scale)) * (1.0 / EDGES)
                index_out[j, k, down, :] = index
                segment_out[j, k, down, :] = segment

    each_strip(strips, one_strip)


FIELD_UNIT = float(1 << 20) / 17.5


def sweep_kernel(*refs, strips, blocks):
    terms = refs[:strips]
    index, segment, weight, disp, out = refs[strips : strips + 5]
    rows, base, raw, field, last_rows = refs[strips + 5 :]
    me = lax.axis_index("strip")
    core = lax.axis_index("feat")
    groups = ROWS_WIN // 4
    parts = ROWS_WIN // 8
    lane = lane_ids(8)
    rows[...] = jnp.zeros_like(rows)
    raw[...] = jnp.zeros_like(raw)
    field[0] = jnp.zeros_like(field[0])
    field[strips + 1] = jnp.zeros_like(field[0])

    for d in range(strips):
        j = lax.rem(lax.axis_index("strip") + d, strips)
        for q in range(4):
            fill_rows(rows, terms[d][q * blocks : (q + 1) * blocks, :])

            def put(w, value, q=q, j=j):
                base[j, q, pl.ds(w, groups, stride=4), :] = value

            to_windows(rows, put)
        words = packed([base[j, c] * FIELD_UNIT for c in range(3)])
        for q in range(2):
            field[j + 1, q] = words[q]

    def spread(j, v):
        down = slice(8 * v, 8 * v + 8)
        ends = ends_of(j, strips)
        near = [[field[j + g, q, down, :] for q in range(2)] for g in range(3)]
        sums = [jnp.zeros((8, LANES), F32)] * 3
        for k in range(EDGES):
            part = segment[j, k, down, :]
            got = unpacked(picked(near, index[j, k, down, :], part >= 1, part >= 2, ends))
            size = weight[j, k, down, :]
            sums = [s + size * g for s, g in zip(sums, got)]
        return [s * (1.0 / FIELD_UNIT) for s in sums]

    beyond = jnp.where(lane < LANES // 2, lane + KEEP, lane - KEEP) & (LANES - 1)

    def renew(j):
        for v in range(parts):
            for q in range(2):
                at = 8 * v + 8
                before = raw[j, q, at - 1 : at + 7, :]
                behind = raw[j, q, at + 1 : at + 9, :]
                margin = pick(jnp.where(lane < LANES // 2, behind, before), beyond)
                kept = (lane >= REACH) & (lane < LANES - REACH)
                field[j + 1, q, 8 * v : 8 * v + 8, :] = jnp.where(kept, raw[j, q, at : at + 8, :], margin)

    for sweep in range(SWEEPS):
        wanted = SWEEPS - sweep

        def one_strip(j, wanted=wanted):
            for v in range(parts):
                down = slice(8 * v, 8 * v + 8)
                sums = spread(j, v)
                fresh = [base[j, c, down, :] - base[j, 3, down, :] * sums[c] for c in range(3)]
                words = packed([value * FIELD_UNIT for value in fresh])
                for q in range(2):
                    raw[j, q, 8 * v + 8 : 8 * v + 16, :] = words[q]
                if wanted == 1:

                    @pl.when(me == j)
                    def _():
                        for c in range(3):
                            last_rows[c, down, :] = fresh[c]

        def near_strip(j, body, wanted=wanted):
            if strips <= 4 and wanted > 1:
                body(j)
            else:
                pl.when(jnp.abs(me - j) <= wanted)(lambda: body(j))

        each_strip(strips, lambda j: near_strip(j, one_strip))
        each_strip(strips, lambda j: near_strip(j, renew))

    for v in range(parts):
        down = slice(8 * v, 8 * v + 8)
        sums = spread(me, v)
        for c in range(3):
            last_rows[c, down, :] = sums[c] + last_rows[c, down, :]
    wide_lane = lane_ids()
    live = disp[3] > 0.5
    for c in range(3):
        for i in range(3):
            begin = LANES * i - KEEP * i + REACH
            first = last_rows[c, pl.ds(i, groups, stride=4), :]
            second = last_rows[c, pl.ds(i + 1, groups, stride=4), :]
            held = KEEP - (LANES - KEEP) * i
            value = jnp.where(
                wide_lane < held,
                pltpu.roll(first, LANES - begin, 1),
                pltpu.roll(second, (held - REACH) % LANES, 1),
            )
            rows[pl.ds(i, groups, stride=3), :] = value
        rows[0:blocks, :] = disp[c] + jnp.where(live, rows[0:blocks, :], 0.0)
        for at in range(blocks - 1):
            out[c : c + 1, at * LANES : (at + 1) * LANES] = rows[pl.ds(core + at, 1), :]


def takes(microseconds):
    return pl.CostEstimate(flops=int(microseconds * 1.15e9), bytes_accessed=0, transcendentals=0)


def whole_kernel(part, part_far, mass, mass_far, out, mass_out):
    is_first = lax.axis_index("feat") == 0
    blocks = mass.shape[0]
    half = blocks - 1
    wide = part.shape[1]
    out[:, 0:wide] = jnp.where(is_first, part[...], part_far[...])
    out[:, wide:] = jnp.where(is_first, part_far[...], part[...])
    mass_out[0:half, :] = jnp.where(is_first, mass[0:half, :], mass_far[0:half, :])
    mass_out[half:, :] = jnp.where(is_first, mass_far[1:blocks, :], mass[1:blocks, :])


def around(array, axis):
    count = lax.axis_size(axis)
    return [array] + [
        lax.ppermute(array, axis, [((i + d) % count, i) for i in range(count)]) for d in range(1, count)
    ]


def on_device(
    src_pos, src_feat, tgt_pos, tgt_feat, displacement, sigma_sq, seed_target, counts, edges
):
    slots = src_pos.shape[1]
    cands = tgt_pos.shape[1]
    strips = lax.axis_size("strip")
    half = slots // 2
    points = half + LANES
    blocks = points // LANES
    small = pltpu.CompilerParams(vmem_limit_bytes=12 << 20)

    src_other = around(src_feat, "feat")[1]
    tgt_other = around(tgt_feat, "feat")[1]

    geo_rows = 16 * ((14 * blocks + 15) // 16)
    hbm = pl.BlockSpec(memory_space=pltpu.HBM)
    own = (src_pos, displacement, edges)
    scalars = [pltpu.SMEM((1,), jnp.int32), pltpu.SMEM((1,), F32)]
    geo, z, disp = pl.pallas_call(
        geometry_kernel,
        name="geometry",
        out_shape=(
            jax.ShapeDtypeStruct((geo_rows, LANES), BF16),
            jax.ShapeDtypeStruct((5, blocks, LANES), F32),
            jax.ShapeDtypeStruct((4, blocks, LANES), F32),
        ),
        in_specs=[hbm] * 5,
        out_specs=(VMEM,) * 3,
        scratch_shapes=[pltpu.VMEM(array.shape, array.dtype) for array in own]
        + scalars
        + [pltpu.VMEM((geo_rows, LANES), F32), pltpu.SemaphoreType.DMA((5,))],
        compiler_params=pltpu.CompilerParams(vmem_limit_bytes=(64 << 20) - (64 << 10)),
        cost_estimate=takes(2),
    )(*own, counts, sigma_sq)
    geos = around(geo, "strip")

    arrays = (src_pos, displacement, tgt_pos, seed_target.reshape(1, slots))
    features = (src_feat, src_other, tgt_feat, tgt_other)
    tile = 256
    state_rows = 8 * ((5 * blocks + 7) // 8)
    mine = pltpu.VMEM((src_feat.shape[0], points), BF16)
    theirs = pltpu.VMEM(tgt_feat.shape, BF16)
    state = pl.pallas_call(
        functools.partial(score_kernel, chunk=points // 8, tile=tile),
        name="score",
        out_shape=jax.ShapeDtypeStruct((state_rows, LANES), F32),
        in_specs=[hbm] * 9,
        out_specs=VMEM,
        scratch_shapes=scalars[1:]
        + [pltpu.VMEM(array.shape, array.dtype) for array in arrays]
        + [mine, mine, theirs, theirs]
        + [
            pltpu.VMEM((points, LANES), F32),
            pltpu.VMEM((LANES, cands), BF16),
            pltpu.VMEM((cands, LANES), BF16),
            pltpu.VMEM((points, 2 * LANES), BF16),
            pltpu.VMEM((cands // tile, points, tile), F32),
            pltpu.VMEM((points, LANES), F32),
            pltpu.SemaphoreType.DMA((9,)),
        ],
        compiler_params=pltpu.CompilerParams(vmem_limit_bytes=60 << 20),
        cost_estimate=takes(10),
    )(sigma_sq, *arrays, *features)

    shape = (strips, EDGES, ROWS_WIN, LANES)
    index, segment, weight = pl.pallas_call(
        functools.partial(kernels_kernel, strips=strips, blocks=blocks),
        name="neighbours",
        out_shape=(
            jax.ShapeDtypeStruct(shape, jnp.int32),
            jax.ShapeDtypeStruct(shape, jnp.int32),
            jax.ShapeDtypeStruct(shape, F32),
        ),
        in_specs=[VMEM] * strips,
        out_specs=(VMEM,) * 3,
        scratch_shapes=[
            pltpu.VMEM((geo_rows, LANES), F32),
            pltpu.VMEM((ROWS_WIN + 16, LANES), F32),
            pltpu.VMEM(shape, F32),
            pltpu.VMEM((3, ROWS_WIN, LANES), F32),
            pltpu.VMEM((strips + 2, 2, ROWS_WIN, LANES), jnp.int32),
        ],
        compiler_params=small,
        cost_estimate=takes(2),
    )(*geos)

    states = around(state, "cand")
    term_rows = 8 * ((4 * blocks + 7) // 8)
    terms, mass = pl.pallas_call(
        merge_kernel,
        name="merge",
        out_shape=(
            jax.ShapeDtypeStruct((term_rows, LANES), F32),
            jax.ShapeDtypeStruct((blocks, LANES), F32),
        ),
        in_specs=[VMEM] * (1 + len(states)) + [pl.BlockSpec(memory_space=pl.ANY)],
        out_specs=(VMEM, VMEM),
        compiler_params=small,
        cost_estimate=takes(0.5),
    )(z, *states, weight)

    all_terms = around(terms, "strip")
    mass_far = around(mass, "feat")[1]

    part = pl.pallas_call(
        functools.partial(sweep_kernel, strips=strips, blocks=blocks),
        name="sweeps",
        out_shape=jax.ShapeDtypeStruct((3, half), F32),
        in_specs=[VMEM] * (strips + 4),
        out_specs=VMEM,
        scratch_shapes=[
            pltpu.VMEM((ROWS_WIN + 16, LANES), F32),
            pltpu.VMEM((strips, 4, ROWS_WIN, LANES), F32),
            pltpu.VMEM((strips, 2, ROWS_WIN + 16, LANES), jnp.int32),
            pltpu.VMEM((strips + 2, 2, ROWS_WIN, LANES), jnp.int32),
            pltpu.VMEM((3, ROWS_WIN + 8, LANES), F32),
        ],
        compiler_params=small,
        cost_estimate=takes(7),
    )(*all_terms, index, segment, weight, disp)

    new_disp, mass_whole = pl.pallas_call(
        whole_kernel,
        name="whole",
        out_shape=(
            jax.ShapeDtypeStruct((3, slots), F32),
            jax.ShapeDtypeStruct((slots // LANES, LANES), F32),
        ),
        in_specs=[VMEM] * 4,
        out_specs=(VMEM, VMEM),
        compiler_params=small,
        cost_estimate=takes(0.5),
    )(part, around(part, "feat")[1], mass, mass_far)
    return (new_disp, mass_whole.reshape(slots))


def solution(mesh):
    in_specs = (
        P(None, ("groups", "strip")),
        P("feat", ("groups", "strip")),
        P(None, ("groups", "strip", "cand")),
        P("feat", ("groups", "strip", "cand")),
        P(None, ("groups", "strip")),
        P(("groups", "strip")),
        P(("groups", "strip")),
        P(("groups", "strip")),
        P(None, ("groups", "strip")),
    )
    out_specs = (P(None, ("groups", "strip")), P(("groups", "strip")))
    return jax.shard_map(
        on_device, mesh=mesh, in_specs=in_specs, out_specs=out_specs, check_vma=False
    )
```

```python
import functools

import jax
import jax.numpy as jnp
from jax import lax
from jax.experimental import pallas as pl
from jax.experimental.pallas import tpu as pltpu
from jax.sharding import PartitionSpec as P

REACH = 16
SWEEPS = 4
EDGES = 8
SPAN = 2 * REACH + 1
LANES = 128
ROWS_WIN = 24
KEEP = LANES - 2 * REACH

feature_scale = 0.18
tie_gain = 3.0
outlier_level = 1.0
strip_offset = 2.0
kernel_scale = 8.0
coherence = 0.1

LOG2E = 1.4426950408889634
VMEM = pl.BlockSpec(memory_space=pltpu.VMEM)
F32 = jnp.float32
BF16 = jnp.bfloat16


def first_slot(slots):
    return lax.axis_index("feat") * (slots // 2 - LANES)


def three_parts(value):
    first = value.astype(BF16).astype(F32)
    rest = value - first
    second = rest.astype(BF16).astype(F32)
    third = (rest - second).astype(BF16).astype(F32)
    return first, second, third


def lane_ids(rows=1):
    return lax.broadcasted_iota(jnp.int32, (rows, LANES), 1)


def copies_in(sources, targets, done):
    copies = [
        pltpu.make_async_copy(source, target, done.at[n])
        for n, (source, target) in enumerate(zip(sources, targets))
    ]
    for copy in copies:
        copy.start()
    return copies


def geometry_kernel(
    far_pos, far_disp, far_edges, far_counts, far_sigma, geo, z_out, disp_out, src_pos, disp, edges, counts, sigma, rows, done
):
    slots = src_pos.shape[1]
    base = first_slot(slots)
    blocks = z_out.shape[1]
    copies = copies_in(
        [far_pos, far_disp, far_edges, far_counts, far_sigma], [src_pos, disp, edges, counts, sigma], done
    )
    rows[...] = jnp.zeros_like(rows)
    for copy in copies:
        copy.wait()
    for at in range(blocks):
        here = pl.ds(pl.multiple_of(base + at * LANES, LANES), LANES)
        pos = src_pos[:, here]
        move = disp[:, here]
        z = pos + move
        edge = edges[:, here]
        slot = base + at * LANES + lane_ids()
        segment = edge // slots
        local = edge - segment * slots
        away = jnp.clip(local - slot + REACH, 0, SPAN - 1)
        code = (segment * SPAN + away).astype(F32)
        high = pos.astype(BF16).astype(F32)
        low = pos - high
        for k in range(EDGES):
            rows[k * blocks + at : k * blocks + at + 1, :] = code[k : k + 1, :]
        for c in range(3):
            put = (EDGES + c) * blocks + at
            rows[put : put + 1, :] = high[c : c + 1, :]
            put = (EDGES + 3 + c) * blocks + at
            rows[put : put + 1, :] = low[c : c + 1, :]
            z_out[c, at : at + 1, :] = z[c : c + 1, :]
            disp_out[c, at : at + 1, :] = move[c : c + 1, :]
    live = (slot_ids(slots, blocks) < counts[0]).astype(F32)
    z_out[3] = live
    z_out[4] = jnp.full((blocks, LANES), sigma[0], F32)
    disp_out[3] = live
    geo[...] = rows[...].astype(BF16)


def score_kernel(*refs, chunk, tile):
    far, state, near = refs[:9], refs[10], refs[11:20]
    cols, aug, x_cols, left, score, highest, done = refs[20:]
    slots = far[1].shape[1]
    points = cols.shape[0]
    mine = pl.ds(pl.multiple_of(first_slot(slots), LANES), points)
    sources = [*far[:5], far[5].at[:, mine], far[6].at[:, mine], far[7], far[8]]
    copies = copies_in(sources, near, done)
    for copy in copies[:5]:
        copy.wait()
    prepare(*near[:5], cols, aug, x_cols)
    for copy in copies[5:]:
        copy.wait()
    score_all(*near[5:], cols, aug, x_cols, state, left, score, highest, chunk=chunk, tile=tile)


def prepare(sigmas, src_pos, disp, tgt_pos, seeds, cols, aug, x_cols):
    slots = src_pos.shape[1]
    base = first_slot(slots)
    sigma = sigmas[0]
    blocks = cols.shape[0] // LANES
    cands = tgt_pos.shape[1]
    offset = lax.axis_index("cand") * cands
    scale = 1.0 / (sigma * feature_scale)
    for at in range(blocks):
        here = pl.ds(pl.multiple_of(base + at * LANES, LANES), LANES)
        z = src_pos[:, here] + disp[:, here]
        first, second, third = three_parts(z * scale)
        norm = jnp.sum(z * z, axis=0, keepdims=True) * (0.5 / sigma)
        level = (norm + outlier_level) * LOG2E
        seed = (seeds[:, here] - offset).astype(F32)
        ones = jnp.ones((3, LANES), F32)
        tile = jnp.concatenate(
            [first, first, second, second, first, third, ones, seed, level]
            + [jnp.zeros((9, LANES), F32)],
            axis=0,
        )
        cols[at * LANES : (at + 1) * LANES, :] = jnp.concatenate(
            [tile.T, jnp.zeros((LANES, LANES - 32), F32)], axis=1
        )
    for at in range(cands // LANES):
        here = pl.ds(at * LANES, LANES)
        x = tgt_pos[:, here]
        first, second, third = three_parts(x)
        norm = jnp.sum(x * x, axis=0, keepdims=True) * (-0.5 * scale)
        parts = three_parts(norm)
        aug[:, here] = jnp.concatenate(
            [first, second, first, second, third, first, *parts, jnp.zeros((LANES - 21, LANES), F32)],
            axis=0,
        ).astype(BF16)
        one = jnp.ones((1, LANES), F32)
        gap = jnp.zeros((5, LANES), F32)
        tile = jnp.concatenate(
            [first, one, gap[:4], second, gap, third, gap, jnp.zeros((8, LANES), F32)], axis=0
        )
        x_cols[at * LANES : (at + 1) * LANES, :] = jnp.concatenate(
            [tile.T, jnp.zeros((LANES, LANES - 32), F32)], axis=1
        ).astype(BF16)


def score_all(src_own, src_other, tgt_own, tgt_other, cols, aug, x_cols, state, left, score, highest, *, chunk, tile):
    points = cols.shape[0]
    blocks = points // LANES
    cands = aug.shape[1]
    half = src_own.shape[0]
    for at in range(blocks):
        down = slice(at * LANES, (at + 1) * LANES)
        both = jnp.concatenate([src_own[:, down], src_other[:, down]], axis=0)
        left[down, 0 : 2 * half] = both.T
        left[down, 2 * half :] = cols[down, :].astype(BF16)
    tiles = cands // tile
    per = tile // LANES
    for t in range(tiles):
        across = slice(t * tile, (t + 1) * tile)
        right = jnp.concatenate([tgt_own[:, across], tgt_other[:, across], aug[:, across]], axis=0)
        for r in range(0, points, chunk):
            product = jnp.dot(left[r : r + chunk, :], right, preferred_element_type=F32)
            score[t, r : r + chunk] = product
            top = product[:, :LANES]
            for q in range(1, per):
                top = jnp.maximum(top, product[:, q * LANES : (q + 1) * LANES])
            highest[r : r + chunk] = top if t == 0 else jnp.maximum(highest[r : r + chunk], top)
    ids = lax.broadcasted_iota(jnp.int32, (1, tile), 1).astype(F32)
    state[...] = jnp.zeros_like(state)
    for r in range(0, points, chunk):
        seed = cols[r : r + chunk, 21:22]
        level = cols[r : r + chunk, 22:23]
        top = jnp.max(highest[r : r + chunk], axis=1, keepdims=True) * (feature_scale * LOG2E)
        peak = jnp.maximum(top, level)
        tied = peak - tie_gain * LOG2E
        total = jnp.zeros((chunk, LANES), F32)
        for t in range(tiles):
            shift = jnp.where(ids + float(t * tile) == seed, tied, peak)
            weight = jnp.exp2(score[t, r : r + chunk] * (feature_scale * LOG2E) - shift)
            high = weight.astype(BF16)
            low = (weight - high.astype(F32)).astype(BF16)
            x = x_cols[t * tile : (t + 1) * tile, :]
            total += jnp.dot(high, x, preferred_element_type=F32)
            total += jnp.dot(low, x, preferred_element_type=F32)
        total = jnp.where(lane_ids() == 4, peak, total)
        highest[r : r + chunk] = total
    for at in range(blocks):
        flat = highest[at * LANES : (at + 1) * LANES, :].T
        summed = flat[0:8] + flat[8:16] + flat[16:24]
        for q in range(5):
            state[q * blocks + at : q * blocks + at + 1, :] = summed[q : q + 1, :]


def slot_ids(slots, blocks):
    rows = lax.broadcasted_iota(jnp.int32, (blocks, LANES), 0)
    return first_slot(slots) + LANES * rows + lane_ids(blocks)


def own_kernel(state, z_ref, geo, out, geo_out):
    geo_out[...] = geo[...]
    blocks = z_ref.shape[1]
    for q in range(5):
        out[q] = state[q * blocks : (q + 1) * blocks, :]
    z = [z_ref[c] for c in range(3)]
    sigma = z_ref[4]
    for c in range(3):
        out[5 + c] = z[c]
    norm = (z[0] * z[0] + z[1] * z[1] + z[2] * z[2]) * (0.5 / sigma)
    out[8] = (norm + outlier_level) * LOG2E
    out[9] = z_ref[3]
    out[10] = sigma


def merge_kernel(own, *refs):
    *others, terms, mass_out = refs
    blocks = own.shape[1]
    states = [[own[q] for q in range(5)]]
    for ref in others:
        states.append([ref[q * blocks : (q + 1) * blocks, :] for q in range(5)])
    peak = states[0][4]
    for state in states[1:]:
        peak = jnp.maximum(peak, state[4])
    sums = [jnp.zeros((blocks, LANES), F32)] * 4
    for state in states:
        factor = jnp.exp2(state[4] - peak)
        sums = [s + state[q] * factor for q, s in enumerate(sums)]
    denom = sums[3] + jnp.exp2(own[8] - peak)
    each = own[9] / denom
    mass = sums[3] * each
    inverse = 1.0 / (mass + coherence * own[10])
    terms[...] = jnp.zeros_like(terms)
    for c in range(3):
        terms[c * blocks : (c + 1) * blocks, :] = (sums[c] * each - mass * own[5 + c]) * inverse
    terms[3 * blocks : 4 * blocks, :] = mass * inverse
    mass_out[...] = mass


def to_windows(rows, put):
    lane = lane_ids()
    groups = ROWS_WIN // 4
    for w, begin in enumerate((-REACH, KEEP - REACH, 2 * KEEP - REACH, 3 * KEEP - REACH)):
        row = begin // LANES
        start = begin - row * LANES
        first = rows[pl.ds(8 + row, groups, stride=3), :]
        second = rows[pl.ds(9 + row, groups, stride=3), :]
        put(w, pltpu.roll(jnp.where(lane >= start, first, second), LANES - start, 1))


def fill_rows(rows, values):
    blocks = values.shape[0]
    rows[8 : 8 + blocks, :] = values


def pick(value, index):
    return jnp.take_along_axis(value, index, axis=1, mode="promise_in_bounds")


def each_strip(count, body):
    if count <= 4:
        for j in range(count):
            body(j)
    else:
        lax.fori_loop(0, count, lambda j, c: (body(j), c)[1], 0)


def packed(values):
    first, second, third = (value.astype(jnp.int32) for value in values)
    third = third + (1 << 20)
    return (first << 11) + (third >> 10), (second << 11) + (third & 1023)


def unpacked(words):
    first, second = words
    third = ((first & 2047) << 10) + (second & 1023) - (1 << 20)
    return [value.astype(F32) for value in (first >> 11, second >> 11, third)]


def picked(words, index, later, last, ends):
    low, high = ends
    got = []
    for w in range(len(words[1])):
        value = pick(words[1][w], index)
        if not low:
            value = jnp.where(later, value, pick(words[0][w], index))
        if not high:
            value = jnp.where(last, pick(words[2][w], index), value)
        got.append(value)
    return got


def ends_of(j, strips):
    return (j == 0, j == strips - 1) if isinstance(j, int) else (False, False)


def kernels_kernel(*refs, strips, blocks):
    geos = refs[:strips]
    index_out, segment_out, weight_out, wide, rows, codes, raw, places = refs[strips:]
    groups = ROWS_WIN // 4
    lane = lane_ids(8)
    rows[...] = jnp.zeros_like(rows)
    places[0] = jnp.zeros_like(places[0])
    places[strips + 1] = jnp.zeros_like(places[0])
    unit = float(1 << 19)

    for d in range(strips):
        wide[...] = geos[d][...].astype(F32)
        j = lax.rem(lax.axis_index("strip") + strips - d, strips)

        for k in range(EDGES):
            fill_rows(rows, wide[k * blocks : (k + 1) * blocks, :])

            def put_code(w, value, k=k, j=j):
                codes[j, k, pl.ds(w, groups, stride=4), :] = value

            to_windows(rows, put_code)
        for c in range(3):
            at = (EDGES + c) * blocks
            more = at + 3 * blocks
            fill_rows(rows, wide[at : at + blocks, :] + wide[more : more + blocks, :])

            def put_place(w, value, c=c):
                raw[c, pl.ds(w, groups, stride=4), :] = value

            to_windows(rows, put_place)
        for q, word in enumerate(packed([raw[c] * unit for c in range(3)])):
            places[j + 1, q] = word

    def one_strip(j):
        ends = ends_of(j, strips)
        for v in range(ROWS_WIN // 8):
            down = slice(8 * v, 8 * v + 8)
            near = [[places[j + g, q, down, :] for q in range(2)] for g in range(3)]
            own = unpacked(near[1])
            for k in range(EDGES):
                code = codes[j, k, down, :].astype(jnp.int32)
                later = code >= SPAN
                last = code >= 2 * SPAN
                segment = later.astype(jnp.int32) + last.astype(jnp.int32)
                index = jnp.clip(lane + code - segment * SPAN - REACH, 0, LANES - 1)
                got = unpacked(picked(near, index, later, last, ends))
                gaps = [(own[c] - got[c]) * (1.0 / unit) for c in range(3)]
                gaps[0] = gaps[0] - strip_offset * (segment - 1).astype(F32)
                total = gaps[0] * gaps[0] + gaps[1] * gaps[1] + gaps[2] * gaps[2]
                weight_out[j, k, down, :] = jnp.exp(total * (-0.5 / kernel_scale)) * (1.0 / EDGES)
                index_out[j, k, down, :] = index
                segment_out[j, k, down, :] = segment

    each_strip(strips, one_strip)


FIELD_UNIT = float(1 << 20) / 17.5


def sweep_kernel(*refs, strips, blocks):
    terms = refs[:strips]
    index, segment, weight, disp, out = refs[strips : strips + 5]
    rows, base, raw, field, last_rows = refs[strips + 5 :]
    me = lax.axis_index("strip")
    core = lax.axis_index("feat")
    groups = ROWS_WIN // 4
    parts = ROWS_WIN // 8
    lane = lane_ids(8)
    rows[...] = jnp.zeros_like(rows)
    raw[...] = jnp.zeros_like(raw)
    field[0] = jnp.zeros_like(field[0])
    field[strips + 1] = jnp.zeros_like(field[0])

    for d in range(strips):
        j = lax.rem(lax.axis_index("strip") + strips - d, strips)
        for q in range(4):
            fill_rows(rows, terms[d][q * blocks : (q + 1) * blocks, :])

            def put(w, value, q=q, j=j):
                base[j, q, pl.ds(w, groups, stride=4), :] = value

            to_windows(rows, put)
        words = packed([base[j, c] * FIELD_UNIT for c in range(3)])
        for q in range(2):
            field[j + 1, q] = words[q]

    def spread(j, v):
        down = slice(8 * v, 8 * v + 8)
        ends = ends_of(j, strips)
        near = [[field[j + g, q, down, :] for q in range(2)] for g in range(3)]
        sums = [jnp.zeros((8, LANES), F32)] * 3
        for k in range(EDGES):
            part = segment[j, k, down, :]
            got = unpacked(picked(near, index[j, k, down, :], part >= 1, part >= 2, ends))
            size = weight[j, k, down, :]
            sums = [s + size * g for s, g in zip(sums, got)]
        return [s * (1.0 / FIELD_UNIT) for s in sums]

    beyond = jnp.where(lane < LANES // 2, lane + KEEP, lane - KEEP) & (LANES - 1)

    def renew(j):
        for v in range(parts):
            for q in range(2):
                at = 8 * v + 8
                before = raw[j, q, at - 1 : at + 7, :]
                behind = raw[j, q, at + 1 : at + 9, :]
                margin = pick(jnp.where(lane < LANES // 2, behind, before), beyond)
                kept = (lane >= REACH) & (lane < LANES - REACH)
                field[j + 1, q, 8 * v : 8 * v + 8, :] = jnp.where(kept, raw[j, q, at : at + 8, :], margin)

    for sweep in range(SWEEPS):
        wanted = SWEEPS - sweep

        def one_strip(j, wanted=wanted):
            for v in range(parts):
                down = slice(8 * v, 8 * v + 8)
                sums = spread(j, v)
                fresh = [base[j, c, down, :] - base[j, 3, down, :] * sums[c] for c in range(3)]
                words = packed([value * FIELD_UNIT for value in fresh])
                for q in range(2):
                    raw[j, q, 8 * v + 8 : 8 * v + 16, :] = words[q]
                if wanted == 1:

                    @pl.when(me == j)
                    def _():
                        for c in range(3):
                            last_rows[c, down, :] = fresh[c]

        def near_strip(j, body, wanted=wanted):
            if strips <= 4 and wanted > 1:
                body(j)
            else:
                pl.when(jnp.abs(me - j) <= wanted)(lambda: body(j))

        each_strip(strips, lambda j: near_strip(j, one_strip))
        each_strip(strips, lambda j: near_strip(j, renew))

    for v in range(parts):
        down = slice(8 * v, 8 * v + 8)
        sums = spread(me, v)
        for c in range(3):
            last_rows[c, down, :] = sums[c] + last_rows[c, down, :]
    wide_lane = lane_ids()
    live = disp[3] > 0.5
    for c in range(3):
        for i in range(3):
            begin = LANES * i - KEEP * i + REACH
            first = last_rows[c, pl.ds(i, groups, stride=4), :]
            second = last_rows[c, pl.ds(i + 1, groups, stride=4), :]
            held = KEEP - (LANES - KEEP) * i
            value = jnp.where(
                wide_lane < held,
                pltpu.roll(first, LANES - begin, 1),
                pltpu.roll(second, (held - REACH) % LANES, 1),
            )
            rows[pl.ds(i, groups, stride=3), :] = value
        rows[0:blocks, :] = disp[c] + jnp.where(live, rows[0:blocks, :], 0.0)
        for at in range(blocks - 1):
            out[c : c + 1, at * LANES : (at + 1) * LANES] = rows[pl.ds(core + at, 1), :]


def takes(microseconds):
    return pl.CostEstimate(flops=int(microseconds * 1.15e9), bytes_accessed=0, transcendentals=0)


def whole_kernel(part, part_far, mass, mass_far, out, mass_out):
    is_first = lax.axis_index("feat") == 0
    blocks = mass.shape[0]
    half = blocks - 1
    wide = part.shape[1]
    out[:, 0:wide] = jnp.where(is_first, part[...], part_far[...])
    out[:, wide:] = jnp.where(is_first, part_far[...], part[...])
    mass_out[0:half, :] = jnp.where(is_first, mass[0:half, :], mass_far[0:half, :])
    mass_out[half:, :] = jnp.where(is_first, mass_far[1:blocks, :], mass[1:blocks, :])


def around(array, axis):
    count = lax.axis_size(axis)
    return [array] + [
        lax.ppermute(array, axis, [(i, (i + d) % count) for i in range(count)]) for d in range(1, count)
    ]


def on_device(
    src_pos, src_feat, tgt_pos, tgt_feat, displacement, sigma_sq, seed_target, counts, edges
):
    slots = src_pos.shape[1]
    cands = tgt_pos.shape[1]
    strips = lax.axis_size("strip")
    half = slots // 2
    points = half + LANES
    blocks = points // LANES
    small = pltpu.CompilerParams(vmem_limit_bytes=12 << 20)

    src_other = around(src_feat, "feat")[1]
    tgt_other = around(tgt_feat, "feat")[1]

    geo_rows = 16 * ((14 * blocks + 15) // 16)
    hbm = pl.BlockSpec(memory_space=pltpu.HBM)
    own = (src_pos, displacement, edges)
    scalars = [pltpu.SMEM((1,), jnp.int32), pltpu.SMEM((1,), F32)]
    geo, z, disp = pl.pallas_call(
        geometry_kernel,
        name="geometry",
        out_shape=(
            jax.ShapeDtypeStruct((geo_rows, LANES), BF16),
            jax.ShapeDtypeStruct((5, blocks, LANES), F32),
            jax.ShapeDtypeStruct((4, blocks, LANES), F32),
        ),
        in_specs=[hbm] * 5,
        out_specs=(VMEM,) * 3,
        scratch_shapes=[pltpu.VMEM(array.shape, array.dtype) for array in own]
        + scalars
        + [pltpu.VMEM((geo_rows, LANES), F32), pltpu.SemaphoreType.DMA((5,))],
        compiler_params=pltpu.CompilerParams(vmem_limit_bytes=(64 << 20) - (64 << 10)),
        cost_estimate=takes(2),
    )(*own, counts, sigma_sq)
    arrays = (src_pos, displacement, tgt_pos, seed_target.reshape(1, slots))
    features = (src_feat, src_other, tgt_feat, tgt_other)
    tile = 256
    state_rows = 8 * ((5 * blocks + 7) // 8)
    mine = pltpu.VMEM((src_feat.shape[0], points), BF16)
    theirs = pltpu.VMEM(tgt_feat.shape, BF16)
    state = pl.pallas_call(
        functools.partial(score_kernel, chunk=points // 8, tile=tile),
        name="score",
        out_shape=jax.ShapeDtypeStruct((state_rows, LANES), F32),
        in_specs=[hbm] * 9 + [pl.BlockSpec(memory_space=pl.ANY)],
        out_specs=VMEM,
        scratch_shapes=scalars[1:]
        + [pltpu.VMEM(array.shape, array.dtype) for array in arrays]
        + [mine, mine, theirs, theirs]
        + [
            pltpu.VMEM((points, LANES), F32),
            pltpu.VMEM((LANES, cands), BF16),
            pltpu.VMEM((cands, LANES), BF16),
            pltpu.VMEM((points, 2 * LANES), BF16),
            pltpu.VMEM((cands // tile, points, tile), F32),
            pltpu.VMEM((points, LANES), F32),
            pltpu.SemaphoreType.DMA((9,)),
        ],
        compiler_params=pltpu.CompilerParams(vmem_limit_bytes=60 << 20),
        cost_estimate=takes(10),
    )(sigma_sq, *arrays, *features, z)

    own, geo = pl.pallas_call(
        own_kernel,
        name="own",
        out_shape=(
            jax.ShapeDtypeStruct((11, blocks, LANES), F32),
            jax.ShapeDtypeStruct((geo_rows, LANES), BF16),
        ),
        in_specs=[VMEM] * 3,
        out_specs=(VMEM, VMEM),
        compiler_params=small,
        cost_estimate=takes(0.5),
    )(state, z, geo)
    geos = around(geo, "strip")
    shape = (strips, EDGES, ROWS_WIN, LANES)
    index, segment, weight = pl.pallas_call(
        functools.partial(kernels_kernel, strips=strips, blocks=blocks),
        name="neighbours",
        out_shape=(
            jax.ShapeDtypeStruct(shape, jnp.int32),
            jax.ShapeDtypeStruct(shape, jnp.int32),
            jax.ShapeDtypeStruct(shape, F32),
        ),
        in_specs=[VMEM] * strips,
        out_specs=(VMEM,) * 3,
        scratch_shapes=[
            pltpu.VMEM((geo_rows, LANES), F32),
            pltpu.VMEM((ROWS_WIN + 16, LANES), F32),
            pltpu.VMEM(shape, F32),
            pltpu.VMEM((3, ROWS_WIN, LANES), F32),
            pltpu.VMEM((strips + 2, 2, ROWS_WIN, LANES), jnp.int32),
        ],
        compiler_params=small,
        cost_estimate=takes(2),
    )(*geos)

    states = around(state, "cand")
    term_rows = 8 * ((4 * blocks + 7) // 8)
    terms, mass = pl.pallas_call(
        merge_kernel,
        name="merge",
        out_shape=(
            jax.ShapeDtypeStruct((term_rows, LANES), F32),
            jax.ShapeDtypeStruct((blocks, LANES), F32),
        ),
        in_specs=[VMEM] * len(states),
        out_specs=(VMEM, VMEM),
        compiler_params=small,
        cost_estimate=takes(0.5),
    )(own, *states[1:])

    all_terms = around(terms, "strip")
    mass_far = around(mass, "feat")[1]

    part = pl.pallas_call(
        functools.partial(sweep_kernel, strips=strips, blocks=blocks),
        name="sweeps",
        out_shape=jax.ShapeDtypeStruct((3, half), F32),
        in_specs=[VMEM] * (strips + 4),
        out_specs=VMEM,
        scratch_shapes=[
            pltpu.VMEM((ROWS_WIN + 16, LANES), F32),
            pltpu.VMEM((strips, 4, ROWS_WIN, LANES), F32),
            pltpu.VMEM((strips, 2, ROWS_WIN + 16, LANES), jnp.int32),
            pltpu.VMEM((strips + 2, 2, ROWS_WIN, LANES), jnp.int32),
            pltpu.VMEM((3, ROWS_WIN + 8, LANES), F32),
        ],
        compiler_params=small,
        cost_estimate=takes(7),
    )(*all_terms, index, segment, weight, disp)

    new_disp, mass_whole = pl.pallas_call(
        whole_kernel,
        name="whole",
        out_shape=(
            jax.ShapeDtypeStruct((3, slots), F32),
            jax.ShapeDtypeStruct((slots // LANES, LANES), F32),
        ),
        in_specs=[VMEM] * 4,
        out_specs=(VMEM, VMEM),
        compiler_params=small,
        cost_estimate=takes(0.5),
    )(part, around(part, "feat")[1], mass, mass_far)
    return (new_disp, mass_whole.reshape(slots))


def solution(mesh):
    in_specs = (
        P(None, ("groups", "strip")),
        P("feat", ("groups", "strip")),
        P(None, ("groups", "strip", "cand")),
        P("feat", ("groups", "strip", "cand")),
        P(None, ("groups", "strip")),
        P(("groups", "strip")),
        P(("groups", "strip")),
        P(("groups", "strip")),
        P(None, ("groups", "strip")),
    )
    out_specs = (P(None, ("groups", "strip")), P(("groups", "strip")))
    return jax.shard_map(
        on_device, mesh=mesh, in_specs=in_specs, out_specs=out_specs, check_vma=False
    )
```

```python
import functools

import jax
import jax.numpy as jnp
from jax import lax
from jax.experimental import pallas as pl
from jax.experimental.pallas import tpu as pltpu
from jax.sharding import PartitionSpec as P

REACH = 16
SWEEPS = 4
EDGES = 8
SPAN = 2 * REACH + 1
LANES = 128
ROWS_WIN = 24
KEEP = LANES - 2 * REACH

feature_scale = 0.18
tie_gain = 3.0
outlier_level = 1.0
strip_offset = 2.0
kernel_scale = 8.0
coherence = 0.1

LOG2E = 1.4426950408889634
VMEM = pl.BlockSpec(memory_space=pltpu.VMEM)
F32 = jnp.float32
BF16 = jnp.bfloat16


def first_slot(slots):
    return lax.axis_index("feat") * (slots // 2 - LANES)


def three_parts(value):
    first = value.astype(BF16).astype(F32)
    rest = value - first
    second = rest.astype(BF16).astype(F32)
    third = (rest - second).astype(BF16).astype(F32)
    return first, second, third


def lane_ids(rows=1):
    return lax.broadcasted_iota(jnp.int32, (rows, LANES), 1)


def copies_in(sources, targets, done):
    copies = [
        pltpu.make_async_copy(source, target, done.at[n])
        for n, (source, target) in enumerate(zip(sources, targets))
    ]
    for copy in copies:
        copy.start()
    return copies


def geometry_kernel(
    far_pos, far_disp, far_edges, far_counts, far_sigma, geo, z_out, disp_out, src_pos, disp, edges, counts, sigma, rows, done
):
    slots = src_pos.shape[1]
    base = first_slot(slots)
    blocks = z_out.shape[1]
    copies = copies_in(
        [far_pos, far_disp, far_edges, far_counts, far_sigma], [src_pos, disp, edges, counts, sigma], done
    )
    rows[...] = jnp.zeros_like(rows)
    for copy in copies:
        copy.wait()
    for at in range(blocks):
        here = pl.ds(pl.multiple_of(base + at * LANES, LANES), LANES)
        pos = src_pos[:, here]
        move = disp[:, here]
        z = pos + move
        edge = edges[:, here]
        slot = base + at * LANES + lane_ids()
        segment = edge // slots
        local = edge - segment * slots
        away = jnp.clip(local - slot + REACH, 0, SPAN - 1)
        code = (segment * SPAN + away).astype(F32)
        high = pos.astype(BF16).astype(F32)
        low = pos - high
        for k in range(EDGES):
            rows[k * blocks + at : k * blocks + at + 1, :] = code[k : k + 1, :]
        for c in range(3):
            put = (EDGES + c) * blocks + at
            rows[put : put + 1, :] = high[c : c + 1, :]
            put = (EDGES + 3 + c) * blocks + at
            rows[put : put + 1, :] = low[c : c + 1, :]
            z_out[c, at : at + 1, :] = z[c : c + 1, :]
            disp_out[c, at : at + 1, :] = move[c : c + 1, :]
    live = (slot_ids(slots, blocks) < counts[0]).astype(F32)
    z_out[3] = live
    z_out[4] = jnp.full((blocks, LANES), sigma[0], F32)
    disp_out[3] = live
    geo[...] = rows[...].astype(BF16)


def score_kernel(*refs, chunk, tile):
    far, state, near = refs[:9], refs[10], refs[11:20]
    cols, aug, x_cols, left, score, highest, done = refs[20:]
    slots = far[1].shape[1]
    points = cols.shape[0]
    mine = pl.ds(pl.multiple_of(first_slot(slots), LANES), points)
    sources = [*far[:5], far[5].at[:, mine], far[6].at[:, mine], far[7], far[8]]
    copies = copies_in(sources, near, done)
    for copy in copies[:5]:
        copy.wait()
    prepare(*near[:5], cols, aug, x_cols)
    for copy in copies[5:]:
        copy.wait()
    score_all(*near[5:], cols, aug, x_cols, state, left, score, highest, chunk=chunk, tile=tile)


def prepare(sigmas, src_pos, disp, tgt_pos, seeds, cols, aug, x_cols):
    slots = src_pos.shape[1]
    base = first_slot(slots)
    sigma = sigmas[0]
    blocks = cols.shape[0] // LANES
    cands = tgt_pos.shape[1]
    offset = lax.axis_index("cand") * cands
    scale = 1.0 / (sigma * feature_scale)
    for at in range(blocks):
        here = pl.ds(pl.multiple_of(base + at * LANES, LANES), LANES)
        z = src_pos[:, here] + disp[:, here]
        first, second, third = three_parts(z * scale)
        norm = jnp.sum(z * z, axis=0, keepdims=True) * (0.5 / sigma)
        level = (norm + outlier_level) * LOG2E
        seed = (seeds[:, here] - offset).astype(F32)
        ones = jnp.ones((3, LANES), F32)
        tile = jnp.concatenate(
            [first, first, second, second, first, third, ones, seed, level]
            + [jnp.zeros((9, LANES), F32)],
            axis=0,
        )
        cols[at * LANES : (at + 1) * LANES, :] = jnp.concatenate(
            [tile.T, jnp.zeros((LANES, LANES - 32), F32)], axis=1
        )
    for at in range(cands // LANES):
        here = pl.ds(at * LANES, LANES)
        x = tgt_pos[:, here]
        first, second, third = three_parts(x)
        norm = jnp.sum(x * x, axis=0, keepdims=True) * (-0.5 * scale)
        parts = three_parts(norm)
        aug[:, here] = jnp.concatenate(
            [first, second, first, second, third, first, *parts, jnp.zeros((LANES - 21, LANES), F32)],
            axis=0,
        ).astype(BF16)
        one = jnp.ones((1, LANES), F32)
        gap = jnp.zeros((5, LANES), F32)
        tile = jnp.concatenate(
            [first, one, gap[:4], second, gap, third, gap, jnp.zeros((8, LANES), F32)], axis=0
        )
        x_cols[at * LANES : (at + 1) * LANES, :] = jnp.concatenate(
            [tile.T, jnp.zeros((LANES, LANES - 32), F32)], axis=1
        ).astype(BF16)


def score_all(src_own, src_other, tgt_own, tgt_other, cols, aug, x_cols, state, left, score, highest, *, chunk, tile):
    points = cols.shape[0]
    blocks = points // LANES
    cands = aug.shape[1]
    half = src_own.shape[0]
    for at in range(blocks):
        down = slice(at * LANES, (at + 1) * LANES)
        both = jnp.concatenate([src_own[:, down], src_other[:, down]], axis=0)
        left[down, 0 : 2 * half] = both.T
        left[down, 2 * half :] = cols[down, :].astype(BF16)
    tiles = cands // tile
    per = tile // LANES
    for t in range(tiles):
        across = slice(t * tile, (t + 1) * tile)
        right = jnp.concatenate([tgt_own[:, across], tgt_other[:, across], aug[:, across]], axis=0)
        for r in range(0, points, chunk):
            product = jnp.dot(left[r : r + chunk, :], right, preferred_element_type=F32)
            score[t, r : r + chunk] = product
            top = product[:, :LANES]
            for q in range(1, per):
                top = jnp.maximum(top, product[:, q * LANES : (q + 1) * LANES])
            highest[r : r + chunk] = top if t == 0 else jnp.maximum(highest[r : r + chunk], top)
    ids = lax.broadcasted_iota(jnp.int32, (1, tile), 1).astype(F32)
    state[...] = jnp.zeros_like(state)
    for r in range(0, points, chunk):
        seed = cols[r : r + chunk, 21:22]
        level = cols[r : r + chunk, 22:23]
        top = jnp.max(highest[r : r + chunk], axis=1, keepdims=True) * (feature_scale * LOG2E)
        peak = jnp.maximum(top, level)
        tied = peak - tie_gain * LOG2E
        total = jnp.zeros((chunk, LANES), F32)
        for t in range(tiles):
            shift = jnp.where(ids + float(t * tile) == seed, tied, peak)
            weight = jnp.exp2(score[t, r : r + chunk] * (feature_scale * LOG2E) - shift)
            x = x_cols[t * tile : (t + 1) * tile, :]
            total += jnp.dot(weight.astype(BF16), x, preferred_element_type=F32)
        total = jnp.where(lane_ids() == 4, peak, total)
        highest[r : r + chunk] = total
    for at in range(blocks):
        flat = highest[at * LANES : (at + 1) * LANES, :].T
        summed = flat[0:8] + flat[8:16] + flat[16:24]
        for q in range(5):
            state[q * blocks + at : q * blocks + at + 1, :] = summed[q : q + 1, :]


def slot_ids(slots, blocks):
    rows = lax.broadcasted_iota(jnp.int32, (blocks, LANES), 0)
    return first_slot(slots) + LANES * rows + lane_ids(blocks)


def own_kernel(state, z_ref, geo, out, geo_out):
    geo_out[...] = geo[...]
    blocks = z_ref.shape[1]
    for q in range(5):
        out[q] = state[q * blocks : (q + 1) * blocks, :]
    z = [z_ref[c] for c in range(3)]
    sigma = z_ref[4]
    for c in range(3):
        out[5 + c] = z[c]
    norm = (z[0] * z[0] + z[1] * z[1] + z[2] * z[2]) * (0.5 / sigma)
    out[8] = (norm + outlier_level) * LOG2E
    out[9] = z_ref[3]
    out[10] = sigma


def merge_kernel(own, *refs):
    *others, terms, mass_out = refs
    blocks = own.shape[1]
    states = [[own[q] for q in range(5)]]
    for ref in others:
        states.append([ref[q * blocks : (q + 1) * blocks, :] for q in range(5)])
    peak = states[0][4]
    for state in states[1:]:
        peak = jnp.maximum(peak, state[4])
    sums = [jnp.zeros((blocks, LANES), F32)] * 4
    for state in states:
        factor = jnp.exp2(state[4] - peak)
        sums = [s + state[q] * factor for q, s in enumerate(sums)]
    denom = sums[3] + jnp.exp2(own[8] - peak)
    each = own[9] / denom
    mass = sums[3] * each
    inverse = 1.0 / (mass + coherence * own[10])
    terms[...] = jnp.zeros_like(terms)
    for c in range(3):
        terms[c * blocks : (c + 1) * blocks, :] = (sums[c] * each - mass * own[5 + c]) * inverse
    terms[3 * blocks : 4 * blocks, :] = mass * inverse
    mass_out[...] = mass


def to_windows(rows, put):
    lane = lane_ids()
    groups = ROWS_WIN // 4
    for w, begin in enumerate((-REACH, KEEP - REACH, 2 * KEEP - REACH, 3 * KEEP - REACH)):
        row = begin // LANES
        start = begin - row * LANES
        first = rows[pl.ds(8 + row, groups, stride=3), :]
        second = rows[pl.ds(9 + row, groups, stride=3), :]
        put(w, pltpu.roll(jnp.where(lane >= start, first, second), LANES - start, 1))


def fill_rows(rows, values):
    blocks = values.shape[0]
    rows[8 : 8 + blocks, :] = values


def pick(value, index):
    return jnp.take_along_axis(value, index, axis=1, mode="promise_in_bounds")


def each_strip(count, body):
    if count <= 4:
        for j in range(count):
            body(j)
    else:
        lax.fori_loop(0, count, lambda j, c: (body(j), c)[1], 0)


def packed(values):
    first, second, third = (value.astype(jnp.int32) for value in values)
    third = third + (1 << 20)
    return (first << 11) + (third >> 10), (second << 11) + (third & 1023)


def unpacked(words):
    first, second = words
    third = ((first & 2047) << 10) + (second & 1023) - (1 << 20)
    return [value.astype(F32) for value in (first >> 11, second >> 11, third)]


def picked(words, index, later, last, ends):
    low, high = ends
    got = []
    for w in range(len(words[1])):
        value = pick(words[1][w], index)
        if not low:
            value = jnp.where(later, value, pick(words[0][w], index))
        if not high:
            value = jnp.where(last, pick(words[2][w], index), value)
        got.append(value)
    return got


def ends_of(j, strips):
    return (j == 0, j == strips - 1) if isinstance(j, int) else (False, False)


def kernels_kernel(*refs, strips, blocks):
    geos = refs[:strips]
    index_out, segment_out, weight_out, wide, rows, codes, raw, places = refs[strips:]
    groups = ROWS_WIN // 4
    lane = lane_ids(8)
    rows[...] = jnp.zeros_like(rows)
    places[0] = jnp.zeros_like(places[0])
    places[strips + 1] = jnp.zeros_like(places[0])
    unit = float(1 << 19)

    for d in range(strips):
        wide[...] = geos[d][...].astype(F32)
        j = lax.rem(lax.axis_index("strip") + strips - d, strips)

        for k in range(EDGES):
            fill_rows(rows, wide[k * blocks : (k + 1) * blocks, :])

            def put_code(w, value, k=k, j=j):
                codes[j, k, pl.ds(w, groups, stride=4), :] = value

            to_windows(rows, put_code)
        for c in range(3):
            at = (EDGES + c) * blocks
            more = at + 3 * blocks
            fill_rows(rows, wide[at : at + blocks, :] + wide[more : more + blocks, :])

            def put_place(w, value, c=c):
                raw[c, pl.ds(w, groups, stride=4), :] = value

            to_windows(rows, put_place)
        for q, word in enumerate(packed([raw[c] * unit for c in range(3)])):
            places[j + 1, q] = word

    def one_strip(j):
        ends = ends_of(j, strips)
        for v in range(ROWS_WIN // 8):
            down = slice(8 * v, 8 * v + 8)
            near = [[places[j + g, q, down, :] for q in range(2)] for g in range(3)]
            own = unpacked(near[1])
            for k in range(EDGES):
                code = codes[j, k, down, :].astype(jnp.int32)
                later = code >= SPAN
                last = code >= 2 * SPAN
                segment = later.astype(jnp.int32) + last.astype(jnp.int32)
                index = jnp.clip(lane + code - segment * SPAN - REACH, 0, LANES - 1)
                got = unpacked(picked(near, index, later, last, ends))
                gaps = [(own[c] - got[c]) * (1.0 / unit) for c in range(3)]
                gaps[0] = gaps[0] - strip_offset * (segment - 1).astype(F32)
                total = gaps[0] * gaps[0] + gaps[1] * gaps[1] + gaps[2] * gaps[2]
                weight_out[j, k, down, :] = jnp.exp(total * (-0.5 / kernel_scale)) * (1.0 / EDGES)
                index_out[j, k, down, :] = index
                segment_out[j, k, down, :] = segment

    each_strip(strips, one_strip)


FIELD_UNIT = float(1 << 20) / 17.5


def sweep_kernel(*refs, strips, blocks):
    terms = refs[:strips]
    index, segment, weight, disp, out = refs[strips : strips + 5]
    rows, base, raw, field, last_rows = refs[strips + 5 :]
    me = lax.axis_index("strip")
    core = lax.axis_index("feat")
    groups = ROWS_WIN // 4
    parts = ROWS_WIN // 8
    lane = lane_ids(8)
    rows[...] = jnp.zeros_like(rows)
    raw[...] = jnp.zeros_like(raw)
    field[0] = jnp.zeros_like(field[0])
    field[strips + 1] = jnp.zeros_like(field[0])

    for d in range(strips):
        j = lax.rem(lax.axis_index("strip") + strips - d, strips)
        for q in range(4):
            fill_rows(rows, terms[d][q * blocks : (q + 1) * blocks, :])

            def put(w, value, q=q, j=j):
                base[j, q, pl.ds(w, groups, stride=4), :] = value

            to_windows(rows, put)
        words = packed([base[j, c] * FIELD_UNIT for c in range(3)])
        for q in range(2):
            field[j + 1, q] = words[q]

    def spread(j, v):
        down = slice(8 * v, 8 * v + 8)
        ends = ends_of(j, strips)
        near = [[field[j + g, q, down, :] for q in range(2)] for g in range(3)]
        sums = [jnp.zeros((8, LANES), F32)] * 3
        for k in range(EDGES):
            part = segment[j, k, down, :]
            got = unpacked(picked(near, index[j, k, down, :], part >= 1, part >= 2, ends))
            size = weight[j, k, down, :]
            sums = [s + size * g for s, g in zip(sums, got)]
        return [s * (1.0 / FIELD_UNIT) for s in sums]

    beyond = jnp.where(lane < LANES // 2, lane + KEEP, lane - KEEP) & (LANES - 1)

    def renew(j):
        for v in range(parts):
            for q in range(2):
                at = 8 * v + 8
                before = raw[j, q, at - 1 : at + 7, :]
                behind = raw[j, q, at + 1 : at + 9, :]
                margin = pick(jnp.where(lane < LANES // 2, behind, before), beyond)
                kept = (lane >= REACH) & (lane < LANES - REACH)
                field[j + 1, q, 8 * v : 8 * v + 8, :] = jnp.where(kept, raw[j, q, at : at + 8, :], margin)

    for sweep in range(SWEEPS):
        wanted = SWEEPS - sweep

        def one_strip(j, wanted=wanted):
            for v in range(parts):
                down = slice(8 * v, 8 * v + 8)
                sums = spread(j, v)
                fresh = [base[j, c, down, :] - base[j, 3, down, :] * sums[c] for c in range(3)]
                words = packed([value * FIELD_UNIT for value in fresh])
                for q in range(2):
                    raw[j, q, 8 * v + 8 : 8 * v + 16, :] = words[q]
                if wanted == 1:

                    @pl.when(me == j)
                    def _():
                        for c in range(3):
                            last_rows[c, down, :] = fresh[c]

        def near_strip(j, body, wanted=wanted):
            if strips <= 4 and wanted > 1:
                body(j)
            else:
                pl.when(jnp.abs(me - j) <= wanted)(lambda: body(j))

        each_strip(strips, lambda j: near_strip(j, one_strip))
        each_strip(strips, lambda j: near_strip(j, renew))

    for v in range(parts):
        down = slice(8 * v, 8 * v + 8)
        sums = spread(me, v)
        for c in range(3):
            last_rows[c, down, :] = sums[c] + last_rows[c, down, :]
    wide_lane = lane_ids()
    live = disp[3] > 0.5
    for c in range(3):
        for i in range(3):
            begin = LANES * i - KEEP * i + REACH
            first = last_rows[c, pl.ds(i, groups, stride=4), :]
            second = last_rows[c, pl.ds(i + 1, groups, stride=4), :]
            held = KEEP - (LANES - KEEP) * i
            value = jnp.where(
                wide_lane < held,
                pltpu.roll(first, LANES - begin, 1),
                pltpu.roll(second, (held - REACH) % LANES, 1),
            )
            rows[pl.ds(i, groups, stride=3), :] = value
        rows[0:blocks, :] = disp[c] + jnp.where(live, rows[0:blocks, :], 0.0)
        for at in range(blocks - 1):
            out[c : c + 1, at * LANES : (at + 1) * LANES] = rows[pl.ds(core + at, 1), :]


def takes(microseconds):
    return pl.CostEstimate(flops=int(microseconds * 1.15e9), bytes_accessed=0, transcendentals=0)


def whole_kernel(part, part_far, mass, mass_far, out, mass_out):
    is_first = lax.axis_index("feat") == 0
    blocks = mass.shape[0]
    half = blocks - 1
    wide = part.shape[1]
    out[:, 0:wide] = jnp.where(is_first, part[...], part_far[...])
    out[:, wide:] = jnp.where(is_first, part_far[...], part[...])
    mass_out[0:half, :] = jnp.where(is_first, mass[0:half, :], mass_far[0:half, :])
    mass_out[half:, :] = jnp.where(is_first, mass_far[1:blocks, :], mass[1:blocks, :])


def around(array, axis):
    count = lax.axis_size(axis)
    return [array] + [
        lax.ppermute(array, axis, [(i, (i + d) % count) for i in range(count)]) for d in range(1, count)
    ]


def on_device(
    src_pos, src_feat, tgt_pos, tgt_feat, displacement, sigma_sq, seed_target, counts, edges
):
    slots = src_pos.shape[1]
    cands = tgt_pos.shape[1]
    strips = lax.axis_size("strip")
    half = slots // 2
    points = half + LANES
    blocks = points // LANES
    small = pltpu.CompilerParams(vmem_limit_bytes=12 << 20)

    src_other = around(src_feat, "feat")[1]
    tgt_other = around(tgt_feat, "feat")[1]

    geo_rows = 16 * ((14 * blocks + 15) // 16)
    hbm = pl.BlockSpec(memory_space=pltpu.HBM)
    own = (src_pos, displacement, edges)
    scalars = [pltpu.SMEM((1,), jnp.int32), pltpu.SMEM((1,), F32)]
    geo, z, disp = pl.pallas_call(
        geometry_kernel,
        name="geometry",
        out_shape=(
            jax.ShapeDtypeStruct((geo_rows, LANES), BF16),
            jax.ShapeDtypeStruct((5, blocks, LANES), F32),
            jax.ShapeDtypeStruct((4, blocks, LANES), F32),
        ),
        in_specs=[hbm] * 5,
        out_specs=(VMEM,) * 3,
        scratch_shapes=[pltpu.VMEM(array.shape, array.dtype) for array in own]
        + scalars
        + [pltpu.VMEM((geo_rows, LANES), F32), pltpu.SemaphoreType.DMA((5,))],
        compiler_params=pltpu.CompilerParams(vmem_limit_bytes=(64 << 20) - (64 << 10)),
        cost_estimate=takes(2),
    )(*own, counts, sigma_sq)
    arrays = (src_pos, displacement, tgt_pos, seed_target.reshape(1, slots))
    features = (src_feat, src_other, tgt_feat, tgt_other)
    tile = 256
    state_rows = 8 * ((5 * blocks + 7) // 8)
    mine = pltpu.VMEM((src_feat.shape[0], points), BF16)
    theirs = pltpu.VMEM(tgt_feat.shape, BF16)
    state = pl.pallas_call(
        functools.partial(score_kernel, chunk=points // 8, tile=tile),
        name="score",
        out_shape=jax.ShapeDtypeStruct((state_rows, LANES), F32),
        in_specs=[hbm] * 9 + [pl.BlockSpec(memory_space=pl.ANY)],
        out_specs=VMEM,
        scratch_shapes=scalars[1:]
        + [pltpu.VMEM(array.shape, array.dtype) for array in arrays]
        + [mine, mine, theirs, theirs]
        + [
            pltpu.VMEM((points, LANES), F32),
            pltpu.VMEM((LANES, cands), BF16),
            pltpu.VMEM((cands, LANES), BF16),
            pltpu.VMEM((points, 2 * LANES), BF16),
            pltpu.VMEM((cands // tile, points, tile), F32),
            pltpu.VMEM((points, LANES), F32),
            pltpu.SemaphoreType.DMA((9,)),
        ],
        compiler_params=pltpu.CompilerParams(vmem_limit_bytes=60 << 20),
        cost_estimate=takes(10),
    )(sigma_sq, *arrays, *features, z)

    own, geo = pl.pallas_call(
        own_kernel,
        name="own",
        out_shape=(
            jax.ShapeDtypeStruct((11, blocks, LANES), F32),
            jax.ShapeDtypeStruct((geo_rows, LANES), BF16),
        ),
        in_specs=[VMEM] * 3,
        out_specs=(VMEM, VMEM),
        compiler_params=small,
        cost_estimate=takes(0.5),
    )(state, z, geo)
    geos = around(geo, "strip")
    shape = (strips, EDGES, ROWS_WIN, LANES)
    index, segment, weight = pl.pallas_call(
        functools.partial(kernels_kernel, strips=strips, blocks=blocks),
        name="neighbours",
        out_shape=(
            jax.ShapeDtypeStruct(shape, jnp.int32),
            jax.ShapeDtypeStruct(shape, jnp.int32),
            jax.ShapeDtypeStruct(shape, F32),
        ),
        in_specs=[VMEM] * strips,
        out_specs=(VMEM,) * 3,
        scratch_shapes=[
            pltpu.VMEM((geo_rows, LANES), F32),
            pltpu.VMEM((ROWS_WIN + 16, LANES), F32),
            pltpu.VMEM(shape, F32),
            pltpu.VMEM((3, ROWS_WIN, LANES), F32),
            pltpu.VMEM((strips + 2, 2, ROWS_WIN, LANES), jnp.int32),
        ],
        compiler_params=small,
        cost_estimate=takes(2),
    )(*geos)

    states = around(state, "cand")
    term_rows = 8 * ((4 * blocks + 7) // 8)
    terms, mass = pl.pallas_call(
        merge_kernel,
        name="merge",
        out_shape=(
            jax.ShapeDtypeStruct((term_rows, LANES), F32),
            jax.ShapeDtypeStruct((blocks, LANES), F32),
        ),
        in_specs=[VMEM] * len(states),
        out_specs=(VMEM, VMEM),
        compiler_params=small,
        cost_estimate=takes(0.5),
    )(own, *states[1:])

    all_terms = around(terms, "strip")
    mass_far = around(mass, "feat")[1]

    part = pl.pallas_call(
        functools.partial(sweep_kernel, strips=strips, blocks=blocks),
        name="sweeps",
        out_shape=jax.ShapeDtypeStruct((3, half), F32),
        in_specs=[VMEM] * (strips + 4),
        out_specs=VMEM,
        scratch_shapes=[
            pltpu.VMEM((ROWS_WIN + 16, LANES), F32),
            pltpu.VMEM((strips, 4, ROWS_WIN, LANES), F32),
            pltpu.VMEM((strips, 2, ROWS_WIN + 16, LANES), jnp.int32),
            pltpu.VMEM((strips + 2, 2, ROWS_WIN, LANES), jnp.int32),
            pltpu.VMEM((3, ROWS_WIN + 8, LANES), F32),
        ],
        compiler_params=small,
        cost_estimate=takes(7),
    )(*all_terms, index, segment, weight, disp)

    new_disp, mass_whole = pl.pallas_call(
        whole_kernel,
        name="whole",
        out_shape=(
            jax.ShapeDtypeStruct((3, slots), F32),
            jax.ShapeDtypeStruct((slots // LANES, LANES), F32),
        ),
        in_specs=[VMEM] * 4,
        out_specs=(VMEM, VMEM),
        compiler_params=small,
        cost_estimate=takes(0.5),
    )(part, around(part, "feat")[1], mass, mass_far)
    return (new_disp, mass_whole.reshape(slots))


def solution(mesh):
    in_specs = (
        P(None, ("groups", "strip")),
        P("feat", ("groups", "strip")),
        P(None, ("groups", "strip", "cand")),
        P("feat", ("groups", "strip", "cand")),
        P(None, ("groups", "strip")),
        P(("groups", "strip")),
        P(("groups", "strip")),
        P(("groups", "strip")),
        P(None, ("groups", "strip")),
    )
    out_specs = (P(None, ("groups", "strip")), P(("groups", "strip")))
    return jax.shard_map(
        on_device, mesh=mesh, in_specs=in_specs, out_specs=out_specs, check_vma=False
    )
```

```python
import functools

import jax
import jax.numpy as jnp
from jax import lax
from jax.experimental import pallas as pl
from jax.experimental.pallas import tpu as pltpu
from jax.sharding import PartitionSpec as P

REACH = 16
SWEEPS = 4
EDGES = 8
SPAN = 2 * REACH + 1
LANES = 128
ROWS_WIN = 24
KEEP = LANES - 2 * REACH

feature_scale = 0.18
tie_gain = 3.0
outlier_level = 1.0
strip_offset = 2.0
kernel_scale = 8.0
coherence = 0.1

LOG2E = 1.4426950408889634
VMEM = pl.BlockSpec(memory_space=pltpu.VMEM)
F32 = jnp.float32
BF16 = jnp.bfloat16


def first_slot(slots):
    return lax.axis_index("feat") * (slots // 2 - LANES)


def three_parts(value):
    first = value.astype(BF16).astype(F32)
    rest = value - first
    second = rest.astype(BF16).astype(F32)
    third = (rest - second).astype(BF16).astype(F32)
    return first, second, third


def lane_ids(rows=1):
    return lax.broadcasted_iota(jnp.int32, (rows, LANES), 1)


def copies_in(sources, targets, done):
    copies = [
        pltpu.make_async_copy(source, target, done.at[n])
        for n, (source, target) in enumerate(zip(sources, targets))
    ]
    for copy in copies:
        copy.start()
    return copies


def hold_kernel(out):
    out[...] = jnp.zeros_like(out)


def bundle_places(blocks):
    at_z = 8 * ((5 * blocks + 7) // 8)
    at_geo = 2 * at_z
    return at_z, at_geo, at_geo + 16 * ((14 * blocks + 15) // 16)


def geometry(src_pos, disp, edges, counts, sigma, bundle, disp_out):
    slots = src_pos.shape[1]
    base = first_slot(slots)
    blocks = disp_out.shape[1]
    at_z, at_geo, _ = bundle_places(blocks)
    bundle[...] = jnp.zeros_like(bundle)
    for at in range(blocks):
        here = pl.ds(pl.multiple_of(base + at * LANES, LANES), LANES)
        pos = src_pos[:, here]
        move = disp[:, here]
        z = pos + move
        edge = edges[:, here]
        slot = base + at * LANES + lane_ids()
        segment = edge // slots
        local = edge - segment * slots
        away = jnp.clip(local - slot + REACH, 0, SPAN - 1)
        code = (segment * SPAN + away).astype(F32)
        high = pos.astype(BF16).astype(F32)
        low = pos - high
        for k in range(EDGES):
            put = at_geo + k * blocks + at
            bundle[put : put + 1, :] = code[k : k + 1, :]
        for c in range(3):
            put = at_geo + (EDGES + c) * blocks + at
            bundle[put : put + 1, :] = high[c : c + 1, :]
            put = at_geo + (EDGES + 3 + c) * blocks + at
            bundle[put : put + 1, :] = low[c : c + 1, :]
            put = at_z + c * blocks + at
            bundle[put : put + 1, :] = z[c : c + 1, :]
            disp_out[c, at : at + 1, :] = move[c : c + 1, :]
    live = (slot_ids(slots, blocks) < counts[0]).astype(F32)
    bundle[at_z + 3 * blocks : at_z + 4 * blocks, :] = live
    bundle[at_z + 4 * blocks : at_z + 5 * blocks, :] = jnp.full((blocks, LANES), sigma[0], F32)
    disp_out[3] = live


def score_kernel(*refs, chunk, tile):
    far, near = refs[:11], refs[15:26]
    state, bundle, disp_out = refs[12:15]
    cols, aug, x_cols, left, score, highest, done = refs[26:]
    slots = far[1].shape[1]
    points = cols.shape[0]
    mine = pl.ds(pl.multiple_of(first_slot(slots), LANES), points)
    sources = [*far[:7], far[7].at[:, mine], far[8].at[:, mine], far[9], far[10]]
    copies = copies_in(sources, near, done)
    for copy in copies[:7]:
        copy.wait()
    sigma, src_pos, disp, tgt_pos, seeds, edges, counts = near[:7]
    prepare(sigma, src_pos, disp, tgt_pos, seeds, cols, aug, x_cols)
    geometry(src_pos, disp, edges, counts, sigma, bundle, disp_out)
    for copy in copies[7:]:
        copy.wait()
    score_all(*near[7:], cols, aug, x_cols, state, left, score, highest, chunk=chunk, tile=tile)
    bundle[0 : state.shape[0], :] = state[...]


def prepare(sigmas, src_pos, disp, tgt_pos, seeds, cols, aug, x_cols):
    slots = src_pos.shape[1]
    base = first_slot(slots)
    sigma = sigmas[0]
    blocks = cols.shape[0] // LANES
    cands = tgt_pos.shape[1]
    offset = lax.axis_index("cand") * cands
    scale = 1.0 / (sigma * feature_scale)
    for at in range(blocks):
        here = pl.ds(pl.multiple_of(base + at * LANES, LANES), LANES)
        z = src_pos[:, here] + disp[:, here]
        first, second, third = three_parts(z * scale)
        norm = jnp.sum(z * z, axis=0, keepdims=True) * (0.5 / sigma)
        level = (norm + outlier_level) * LOG2E
        seed = (seeds[:, here] - offset).astype(F32)
        ones = jnp.ones((3, LANES), F32)
        tile = jnp.concatenate(
            [first, first, second, second, first, third, ones, seed, level]
            + [jnp.zeros((9, LANES), F32)],
            axis=0,
        )
        cols[at * LANES : (at + 1) * LANES, :] = jnp.concatenate(
            [tile.T, jnp.zeros((LANES, LANES - 32), F32)], axis=1
        )
    for at in range(cands // LANES):
        here = pl.ds(at * LANES, LANES)
        x = tgt_pos[:, here]
        first, second, third = three_parts(x)
        norm = jnp.sum(x * x, axis=0, keepdims=True) * (-0.5 * scale)
        parts = three_parts(norm)
        aug[:, here] = jnp.concatenate(
            [first, second, first, second, third, first, *parts, jnp.zeros((LANES - 21, LANES), F32)],
            axis=0,
        ).astype(BF16)
        one = jnp.ones((1, LANES), F32)
        gap = jnp.zeros((5, LANES), F32)
        tile = jnp.concatenate(
            [first, one, gap[:4], second, gap, third, gap, jnp.zeros((8, LANES), F32)], axis=0
        )
        x_cols[at * LANES : (at + 1) * LANES, :] = jnp.concatenate(
            [tile.T, jnp.zeros((LANES, LANES - 32), F32)], axis=1
        ).astype(BF16)


def score_all(src_own, src_other, tgt_own, tgt_other, cols, aug, x_cols, state, left, score, highest, *, chunk, tile):
    points = cols.shape[0]
    blocks = points // LANES
    cands = aug.shape[1]
    half = src_own.shape[0]
    for at in range(blocks):
        down = slice(at * LANES, (at + 1) * LANES)
        both = jnp.concatenate([src_own[:, down], src_other[:, down]], axis=0)
        left[down, 0 : 2 * half] = both.T
        left[down, 2 * half :] = cols[down, :].astype(BF16)
    tiles = cands // tile
    per = tile // LANES
    for t in range(tiles):
        across = slice(t * tile, (t + 1) * tile)
        right = jnp.concatenate([tgt_own[:, across], tgt_other[:, across], aug[:, across]], axis=0)
        for r in range(0, points, chunk):
            product = jnp.dot(left[r : r + chunk, :], right, preferred_element_type=F32)
            score[t, r : r + chunk] = product
            top = product[:, :LANES]
            for q in range(1, per):
                top = jnp.maximum(top, product[:, q * LANES : (q + 1) * LANES])
            highest[r : r + chunk] = top if t == 0 else jnp.maximum(highest[r : r + chunk], top)
    ids = lax.broadcasted_iota(jnp.int32, (1, tile), 1).astype(F32)
    state[...] = jnp.zeros_like(state)
    for r in range(0, points, chunk):
        seed = cols[r : r + chunk, 21:22]
        level = cols[r : r + chunk, 22:23]
        top = jnp.max(highest[r : r + chunk], axis=1, keepdims=True) * (feature_scale * LOG2E)
        peak = jnp.maximum(top, level)
        tied = peak - tie_gain * LOG2E
        total = jnp.zeros((chunk, LANES), F32)
        for t in range(tiles):
            shift = jnp.where(ids + float(t * tile) == seed, tied, peak)
            weight = jnp.exp2(score[t, r : r + chunk] * (feature_scale * LOG2E) - shift)
            x = x_cols[t * tile : (t + 1) * tile, :]
            total += jnp.dot(weight.astype(BF16), x, preferred_element_type=F32)
        total = jnp.where(lane_ids() == 4, peak, total)
        highest[r : r + chunk] = total
    for at in range(blocks):
        flat = highest[at * LANES : (at + 1) * LANES, :].T
        summed = flat[0:8] + flat[8:16] + flat[16:24]
        for q in range(5):
            state[q * blocks + at : q * blocks + at + 1, :] = summed[q : q + 1, :]


def slot_ids(slots, blocks):
    rows = lax.broadcasted_iota(jnp.int32, (blocks, LANES), 0)
    return first_slot(slots) + LANES * rows + lane_ids(blocks)


def own_kernel(bundle, out, geo_out):
    blocks = out.shape[1]
    at_z, at_geo, end = bundle_places(blocks)
    geo_out[...] = bundle[at_geo:end, :].astype(BF16)
    for q in range(5):
        out[q] = bundle[q * blocks : (q + 1) * blocks, :]
    z = [bundle[at_z + c * blocks : at_z + (c + 1) * blocks, :] for c in range(3)]
    sigma = bundle[at_z + 4 * blocks : at_z + 5 * blocks, :]
    for c in range(3):
        out[5 + c] = z[c]
    norm = (z[0] * z[0] + z[1] * z[1] + z[2] * z[2]) * (0.5 / sigma)
    out[8] = (norm + outlier_level) * LOG2E
    out[9] = bundle[at_z + 3 * blocks : at_z + 4 * blocks, :]
    out[10] = sigma


def merge_kernel(own, *refs):
    *others, terms, mass_out = refs
    blocks = own.shape[1]
    states = [[own[q] for q in range(5)]]
    for ref in others:
        states.append([ref[q * blocks : (q + 1) * blocks, :] for q in range(5)])
    peak = states[0][4]
    for state in states[1:]:
        peak = jnp.maximum(peak, state[4])
    sums = [jnp.zeros((blocks, LANES), F32)] * 4
    for state in states:
        factor = jnp.exp2(state[4] - peak)
        sums = [s + state[q] * factor for q, s in enumerate(sums)]
    denom = sums[3] + jnp.exp2(own[8] - peak)
    each = own[9] / denom
    mass = sums[3] * each
    inverse = 1.0 / (mass + coherence * own[10])
    terms[...] = jnp.zeros_like(terms)
    for c in range(3):
        terms[c * blocks : (c + 1) * blocks, :] = (sums[c] * each - mass * own[5 + c]) * inverse
    terms[3 * blocks : 4 * blocks, :] = mass * inverse
    mass_out[...] = mass


def to_windows(rows, put):
    lane = lane_ids()
    groups = ROWS_WIN // 4
    for w, begin in enumerate((-REACH, KEEP - REACH, 2 * KEEP - REACH, 3 * KEEP - REACH)):
        row = begin // LANES
        start = begin - row * LANES
        first = rows[pl.ds(8 + row, groups, stride=3), :]
        second = rows[pl.ds(9 + row, groups, stride=3), :]
        put(w, pltpu.roll(jnp.where(lane >= start, first, second), LANES - start, 1))


def fill_rows(rows, values):
    blocks = values.shape[0]
    rows[8 : 8 + blocks, :] = values


def pick(value, index):
    return jnp.take_along_axis(value, index, axis=1, mode="promise_in_bounds")


def each_strip(count, body):
    if count <= 4:
        for j in range(count):
            body(j)
    else:
        lax.fori_loop(0, count, lambda j, c: (body(j), c)[1], 0)


def packed(values):
    first, second, third = (value.astype(jnp.int32) for value in values)
    third = third + (1 << 20)
    return (first << 11) + (third >> 10), (second << 11) + (third & 1023)


def unpacked(words):
    first, second = words
    third = ((first & 2047) << 10) + (second & 1023) - (1 << 20)
    return [value.astype(F32) for value in (first >> 11, second >> 11, third)]


def picked(words, index, later, last, ends):
    low, high = ends
    got = []
    for w in range(len(words[1])):
        value = pick(words[1][w], index)
        if not low:
            value = jnp.where(later, value, pick(words[0][w], index))
        if not high:
            value = jnp.where(last, pick(words[2][w], index), value)
        got.append(value)
    return got


def ends_of(j, strips):
    return (j == 0, j == strips - 1) if isinstance(j, int) else (False, False)


def kernels_kernel(*refs, strips, blocks):
    geos = refs[:strips]
    index_out, segment_out, weight_out, wide, rows, codes, raw, places = refs[strips:]
    groups = ROWS_WIN // 4
    lane = lane_ids(8)
    rows[...] = jnp.zeros_like(rows)
    places[0] = jnp.zeros_like(places[0])
    places[strips + 1] = jnp.zeros_like(places[0])
    unit = float(1 << 19)

    for d in range(strips):
        wide[...] = geos[d][...].astype(F32)
        j = lax.rem(lax.axis_index("strip") + strips - d, strips)

        for k in range(EDGES):
            fill_rows(rows, wide[k * blocks : (k + 1) * blocks, :])

            def put_code(w, value, k=k, j=j):
                codes[j, k, pl.ds(w, groups, stride=4), :] = value

            to_windows(rows, put_code)
        for c in range(3):
            at = (EDGES + c) * blocks
            more = at + 3 * blocks
            fill_rows(rows, wide[at : at + blocks, :] + wide[more : more + blocks, :])

            def put_place(w, value, c=c):
                raw[c, pl.ds(w, groups, stride=4), :] = value

            to_windows(rows, put_place)
        for q, word in enumerate(packed([raw[c] * unit for c in range(3)])):
            places[j + 1, q] = word

    def one_strip(j):
        ends = ends_of(j, strips)
        for v in range(ROWS_WIN // 8):
            down = slice(8 * v, 8 * v + 8)
            near = [[places[j + g, q, down, :] for q in range(2)] for g in range(3)]
            own = unpacked(near[1])
            for k in range(EDGES):
                code = codes[j, k, down, :].astype(jnp.int32)
                later = code >= SPAN
                last = code >= 2 * SPAN
                segment = later.astype(jnp.int32) + last.astype(jnp.int32)
                index = jnp.clip(lane + code - segment * SPAN - REACH, 0, LANES - 1)
                got = unpacked(picked(near, index, later, last, ends))
                gaps = [(own[c] - got[c]) * (1.0 / unit) for c in range(3)]
                gaps[0] = gaps[0] - strip_offset * (segment - 1).astype(F32)
                total = gaps[0] * gaps[0] + gaps[1] * gaps[1] + gaps[2] * gaps[2]
                weight_out[j, k, down, :] = jnp.exp(total * (-0.5 / kernel_scale)) * (1.0 / EDGES)
                index_out[j, k, down, :] = index
                segment_out[j, k, down, :] = segment

    each_strip(strips, one_strip)


FIELD_UNIT = float(1 << 20) / 17.5


def sweep_kernel(*refs, strips, blocks):
    terms = refs[:strips]
    index, segment, weight, disp, out = refs[strips : strips + 5]
    rows, base, raw, field, last_rows = refs[strips + 5 :]
    me = lax.axis_index("strip")
    core = lax.axis_index("feat")
    groups = ROWS_WIN // 4
    parts = ROWS_WIN // 8
    lane = lane_ids(8)
    rows[...] = jnp.zeros_like(rows)
    raw[...] = jnp.zeros_like(raw)
    field[0] = jnp.zeros_like(field[0])
    field[strips + 1] = jnp.zeros_like(field[0])

    for d in range(strips):
        j = lax.rem(lax.axis_index("strip") + strips - d, strips)
        for q in range(4):
            fill_rows(rows, terms[d][q * blocks : (q + 1) * blocks, :])

            def put(w, value, q=q, j=j):
                base[j, q, pl.ds(w, groups, stride=4), :] = value

            to_windows(rows, put)
        words = packed([base[j, c] * FIELD_UNIT for c in range(3)])
        for q in range(2):
            field[j + 1, q] = words[q]

    def spread(j, v):
        down = slice(8 * v, 8 * v + 8)
        ends = ends_of(j, strips)
        near = [[field[j + g, q, down, :] for q in range(2)] for g in range(3)]
        sums = [jnp.zeros((8, LANES), F32)] * 3
        for k in range(EDGES):
            part = segment[j, k, down, :]
            got = unpacked(picked(near, index[j, k, down, :], part >= 1, part >= 2, ends))
            size = weight[j, k, down, :]
            sums = [s + size * g for s, g in zip(sums, got)]
        return [s * (1.0 / FIELD_UNIT) for s in sums]

    beyond = jnp.where(lane < LANES // 2, lane + KEEP, lane - KEEP) & (LANES - 1)

    def renew(j):
        for v in range(parts):
            for q in range(2):
                at = 8 * v + 8
                before = raw[j, q, at - 1 : at + 7, :]
                behind = raw[j, q, at + 1 : at + 9, :]
                margin = pick(jnp.where(lane < LANES // 2, behind, before), beyond)
                kept = (lane >= REACH) & (lane < LANES - REACH)
                field[j + 1, q, 8 * v : 8 * v + 8, :] = jnp.where(kept, raw[j, q, at : at + 8, :], margin)

    for sweep in range(SWEEPS):
        wanted = SWEEPS - sweep

        def one_strip(j, wanted=wanted):
            for v in range(parts):
                down = slice(8 * v, 8 * v + 8)
                sums = spread(j, v)
                fresh = [base[j, c, down, :] - base[j, 3, down, :] * sums[c] for c in range(3)]
                words = packed([value * FIELD_UNIT for value in fresh])
                for q in range(2):
                    raw[j, q, 8 * v + 8 : 8 * v + 16, :] = words[q]
                if wanted == 1:

                    @pl.when(me == j)
                    def _():
                        for c in range(3):
                            last_rows[c, down, :] = fresh[c]

        def near_strip(j, body, wanted=wanted):
            if strips <= 4 and wanted > 1:
                body(j)
            else:
                pl.when(jnp.abs(me - j) <= wanted)(lambda: body(j))

        each_strip(strips, lambda j: near_strip(j, one_strip))
        each_strip(strips, lambda j: near_strip(j, renew))

    for v in range(parts):
        down = slice(8 * v, 8 * v + 8)
        sums = spread(me, v)
        for c in range(3):
            last_rows[c, down, :] = sums[c] + last_rows[c, down, :]
    wide_lane = lane_ids()
    live = disp[3] > 0.5
    for c in range(3):
        for i in range(3):
            begin = LANES * i - KEEP * i + REACH
            first = last_rows[c, pl.ds(i, groups, stride=4), :]
            second = last_rows[c, pl.ds(i + 1, groups, stride=4), :]
            held = KEEP - (LANES - KEEP) * i
            value = jnp.where(
                wide_lane < held,
                pltpu.roll(first, LANES - begin, 1),
                pltpu.roll(second, (held - REACH) % LANES, 1),
            )
            rows[pl.ds(i, groups, stride=3), :] = value
        rows[0:blocks, :] = disp[c] + jnp.where(live, rows[0:blocks, :], 0.0)
        for at in range(blocks - 1):
            out[c : c + 1, at * LANES : (at + 1) * LANES] = rows[pl.ds(core + at, 1), :]


def takes(microseconds):
    return pl.CostEstimate(flops=int(microseconds * 1.15e9), bytes_accessed=0, transcendentals=0)


def whole_kernel(part, part_far, mass, mass_far, out, mass_out):
    is_first = lax.axis_index("feat") == 0
    blocks = mass.shape[0]
    half = blocks - 1
    wide = part.shape[1]
    out[:, 0:wide] = jnp.where(is_first, part[...], part_far[...])
    out[:, wide:] = jnp.where(is_first, part_far[...], part[...])
    mass_out[0:half, :] = jnp.where(is_first, mass[0:half, :], mass_far[0:half, :])
    mass_out[half:, :] = jnp.where(is_first, mass_far[1:blocks, :], mass[1:blocks, :])


def around(array, axis):
    count = lax.axis_size(axis)
    return [array] + [
        lax.ppermute(array, axis, [(i, (i + d) % count) for i in range(count)]) for d in range(1, count)
    ]


def on_device(
    src_pos, src_feat, tgt_pos, tgt_feat, displacement, sigma_sq, seed_target, counts, edges
):
    slots = src_pos.shape[1]
    cands = tgt_pos.shape[1]
    strips = lax.axis_size("strip")
    half = slots // 2
    points = half + LANES
    blocks = points // LANES
    small = pltpu.CompilerParams(vmem_limit_bytes=12 << 20)

    src_other = around(src_feat, "feat")[1]
    tgt_other = around(tgt_feat, "feat")[1]

    geo_rows = 16 * ((14 * blocks + 15) // 16)
    hbm = pl.BlockSpec(memory_space=pltpu.HBM)
    held = pl.pallas_call(
        hold_kernel,
        name="hold",
        out_shape=jax.ShapeDtypeStruct((8, LANES), F32),
        out_specs=VMEM,
        compiler_params=pltpu.CompilerParams(vmem_limit_bytes=(64 << 20) - (64 << 10)),
        cost_estimate=takes(2),
    )()
    arrays = (src_pos, displacement, tgt_pos, seed_target.reshape(1, slots), edges)
    features = (src_feat, src_other, tgt_feat, tgt_other)
    tile = 256
    state_rows = 8 * ((5 * blocks + 7) // 8)
    mine = pltpu.VMEM((src_feat.shape[0], points), BF16)
    theirs = pltpu.VMEM(tgt_feat.shape, BF16)
    state, bundle, disp = pl.pallas_call(
        functools.partial(score_kernel, chunk=points // 8, tile=tile),
        name="score",
        out_shape=(
            jax.ShapeDtypeStruct((state_rows, LANES), F32),
            jax.ShapeDtypeStruct((bundle_places(blocks)[2], LANES), F32),
            jax.ShapeDtypeStruct((4, blocks, LANES), F32),
        ),
        in_specs=[hbm] * 11 + [pl.BlockSpec(memory_space=pl.ANY)],
        out_specs=(VMEM,) * 3,
        scratch_shapes=[pltpu.SMEM((1,), F32)]
        + [pltpu.VMEM(array.shape, array.dtype) for array in arrays]
        + [pltpu.SMEM((1,), jnp.int32)]
        + [mine, mine, theirs, theirs]
        + [
            pltpu.VMEM((points, LANES), F32),
            pltpu.VMEM((LANES, cands), BF16),
            pltpu.VMEM((cands, LANES), BF16),
            pltpu.VMEM((points, 2 * LANES), BF16),
            pltpu.VMEM((cands // tile, points, tile), F32),
            pltpu.VMEM((points, LANES), F32),
            pltpu.SemaphoreType.DMA((11,)),
        ],
        compiler_params=pltpu.CompilerParams(vmem_limit_bytes=60 << 20),
        cost_estimate=takes(10),
    )(sigma_sq, *arrays, counts, *features, held)

    own, geo = pl.pallas_call(
        own_kernel,
        name="own",
        out_shape=(
            jax.ShapeDtypeStruct((11, blocks, LANES), F32),
            jax.ShapeDtypeStruct((geo_rows, LANES), BF16),
        ),
        in_specs=[VMEM],
        out_specs=(VMEM, VMEM),
        compiler_params=small,
        cost_estimate=takes(0.5),
    )(bundle)
    geos = around(geo, "strip")
    shape = (strips, EDGES, ROWS_WIN, LANES)
    index, segment, weight = pl.pallas_call(
        functools.partial(kernels_kernel, strips=strips, blocks=blocks),
        name="neighbours",
        out_shape=(
            jax.ShapeDtypeStruct(shape, jnp.int32),
            jax.ShapeDtypeStruct(shape, jnp.int32),
            jax.ShapeDtypeStruct(shape, F32),
        ),
        in_specs=[VMEM] * strips,
        out_specs=(VMEM,) * 3,
        scratch_shapes=[
            pltpu.VMEM((geo_rows, LANES), F32),
            pltpu.VMEM((ROWS_WIN + 16, LANES), F32),
            pltpu.VMEM(shape, F32),
            pltpu.VMEM((3, ROWS_WIN, LANES), F32),
            pltpu.VMEM((strips + 2, 2, ROWS_WIN, LANES), jnp.int32),
        ],
        compiler_params=small,
        cost_estimate=takes(2),
    )(*geos)

    states = around(state, "cand")
    term_rows = 8 * ((4 * blocks + 7) // 8)
    terms, mass = pl.pallas_call(
        merge_kernel,
        name="merge",
        out_shape=(
            jax.ShapeDtypeStruct((term_rows, LANES), F32),
            jax.ShapeDtypeStruct((blocks, LANES), F32),
        ),
        in_specs=[VMEM] * len(states),
        out_specs=(VMEM, VMEM),
        compiler_params=small,
        cost_estimate=takes(0.5),
    )(own, *states[1:])

    all_terms = around(terms, "strip")
    mass_far = around(mass, "feat")[1]

    part = pl.pallas_call(
        functools.partial(sweep_kernel, strips=strips, blocks=blocks),
        name="sweeps",
        out_shape=jax.ShapeDtypeStruct((3, half), F32),
        in_specs=[VMEM] * (strips + 4),
        out_specs=VMEM,
        scratch_shapes=[
            pltpu.VMEM((ROWS_WIN + 16, LANES), F32),
            pltpu.VMEM((strips, 4, ROWS_WIN, LANES), F32),
            pltpu.VMEM((strips, 2, ROWS_WIN + 16, LANES), jnp.int32),
            pltpu.VMEM((strips + 2, 2, ROWS_WIN, LANES), jnp.int32),
            pltpu.VMEM((3, ROWS_WIN + 8, LANES), F32),
        ],
        compiler_params=small,
        cost_estimate=takes(7),
    )(*all_terms, index, segment, weight, disp)

    new_disp, mass_whole = pl.pallas_call(
        whole_kernel,
        name="whole",
        out_shape=(
            jax.ShapeDtypeStruct((3, slots), F32),
            jax.ShapeDtypeStruct((slots // LANES, LANES), F32),
        ),
        in_specs=[VMEM] * 4,
        out_specs=(VMEM, VMEM),
        compiler_params=small,
        cost_estimate=takes(0.5),
    )(part, around(part, "feat")[1], mass, mass_far)
    return (new_disp, mass_whole.reshape(slots))


def solution(mesh):
    in_specs = (
        P(None, ("groups", "strip")),
        P("feat", ("groups", "strip")),
        P(None, ("groups", "strip", "cand")),
        P("feat", ("groups", "strip", "cand")),
        P(None, ("groups", "strip")),
        P(("groups", "strip")),
        P(("groups", "strip")),
        P(("groups", "strip")),
        P(None, ("groups", "strip")),
    )
    out_specs = (P(None, ("groups", "strip")), P(("groups", "strip")))
    return jax.shard_map(
        on_device, mesh=mesh, in_specs=in_specs, out_specs=out_specs, check_vma=False
    )
```

```python
import functools

import jax
import jax.numpy as jnp
from jax import lax
from jax.experimental import pallas as pl
from jax.experimental.pallas import tpu as pltpu
from jax.sharding import PartitionSpec as P

REACH = 16
SWEEPS = 4
EDGES = 8
SPAN = 2 * REACH + 1
LANES = 128
ROWS_WIN = 24
KEEP = LANES - 2 * REACH

feature_scale = 0.18
tie_gain = 3.0
outlier_level = 1.0
strip_offset = 2.0
kernel_scale = 8.0
coherence = 0.1

LOG2E = 1.4426950408889634
VMEM = pl.BlockSpec(memory_space=pltpu.VMEM)
F32 = jnp.float32
BF16 = jnp.bfloat16


def first_slot(slots):
    return lax.axis_index("feat") * (slots // 2 - LANES)


def three_parts(value):
    first = value.astype(BF16).astype(F32)
    rest = value - first
    second = rest.astype(BF16).astype(F32)
    third = (rest - second).astype(BF16).astype(F32)
    return first, second, third


def lane_ids(rows=1):
    return lax.broadcasted_iota(jnp.int32, (rows, LANES), 1)


def copies_in(sources, targets, done):
    copies = [
        pltpu.make_async_copy(source, target, done.at[n])
        for n, (source, target) in enumerate(zip(sources, targets))
    ]
    for copy in copies:
        copy.start()
    return copies


def hold_kernel(out):
    out[...] = jnp.zeros_like(out)


def bundle_places(blocks):
    at_z = 8 * ((5 * blocks + 7) // 8)
    at_geo = 2 * at_z
    return at_z, at_geo, at_geo + 16 * ((14 * blocks + 15) // 16)


def geometry(src_pos, disp, edges, counts, sigma, bundle, disp_out):
    slots = src_pos.shape[1]
    base = first_slot(slots)
    blocks = disp_out.shape[1]
    at_z, at_geo, _ = bundle_places(blocks)
    bundle[...] = jnp.zeros_like(bundle)
    for at in range(blocks):
        here = pl.ds(pl.multiple_of(base + at * LANES, LANES), LANES)
        pos = src_pos[:, here]
        move = disp[:, here]
        z = pos + move
        edge = edges[:, here]
        slot = base + at * LANES + lane_ids()
        segment = edge // slots
        local = edge - segment * slots
        away = jnp.clip(local - slot + REACH, 0, SPAN - 1)
        code = (segment * SPAN + away).astype(F32)
        high = pos.astype(BF16).astype(F32)
        low = pos - high
        for k in range(EDGES):
            put = at_geo + k * blocks + at
            bundle[put : put + 1, :] = code[k : k + 1, :]
        for c in range(3):
            put = at_geo + (EDGES + c) * blocks + at
            bundle[put : put + 1, :] = high[c : c + 1, :]
            put = at_geo + (EDGES + 3 + c) * blocks + at
            bundle[put : put + 1, :] = low[c : c + 1, :]
            put = at_z + c * blocks + at
            bundle[put : put + 1, :] = z[c : c + 1, :]
            disp_out[c, at : at + 1, :] = move[c : c + 1, :]
    live = (slot_ids(slots, blocks) < counts[0]).astype(F32)
    bundle[at_z + 3 * blocks : at_z + 4 * blocks, :] = live
    bundle[at_z + 4 * blocks : at_z + 5 * blocks, :] = jnp.full((blocks, LANES), sigma[0], F32)
    disp_out[3] = live


def score_kernel(*refs, chunk, tile):
    far, near = refs[:11], refs[15:26]
    state, bundle, disp_out = refs[12:15]
    cols, aug, x_cols, left, score, highest, done = refs[26:]
    slots = far[1].shape[1]
    points = cols.shape[0]
    mine = pl.ds(pl.multiple_of(first_slot(slots), LANES), points)
    sources = [*far[:7], far[7].at[:, mine], far[8].at[:, mine], far[9], far[10]]
    copies = copies_in(sources, near, done)
    for copy in copies[:7]:
        copy.wait()
    sigma, src_pos, disp, tgt_pos, seeds, edges, counts = near[:7]
    prepare(sigma, src_pos, disp, tgt_pos, seeds, cols, aug, x_cols)
    geometry(src_pos, disp, edges, counts, sigma, bundle, disp_out)
    for copy in copies[7:]:
        copy.wait()
    score_all(*near[7:], cols, aug, x_cols, state, left, score, highest, chunk=chunk, tile=tile)
    bundle[0 : state.shape[0], :] = state[...]


def prepare(sigmas, src_pos, disp, tgt_pos, seeds, cols, aug, x_cols):
    slots = src_pos.shape[1]
    base = first_slot(slots)
    sigma = sigmas[0]
    blocks = cols.shape[0] // LANES
    cands = tgt_pos.shape[1]
    offset = lax.axis_index("cand") * cands
    scale = 1.0 / (sigma * feature_scale)
    for at in range(blocks):
        here = pl.ds(pl.multiple_of(base + at * LANES, LANES), LANES)
        z = src_pos[:, here] + disp[:, here]
        first, second, third = three_parts(z * scale)
        norm = jnp.sum(z * z, axis=0, keepdims=True) * (0.5 / sigma)
        level = (norm + outlier_level) * LOG2E
        seed = (seeds[:, here] - offset).astype(F32)
        ones = jnp.ones((3, LANES), F32)
        tile = jnp.concatenate(
            [first, first, second, second, first, third, ones, seed, level]
            + [jnp.zeros((9, LANES), F32)],
            axis=0,
        )
        cols[at * LANES : (at + 1) * LANES, :] = jnp.concatenate(
            [tile.T, jnp.zeros((LANES, LANES - 32), F32)], axis=1
        )
    for at in range(cands // LANES):
        here = pl.ds(at * LANES, LANES)
        x = tgt_pos[:, here]
        first, second, third = three_parts(x)
        norm = jnp.sum(x * x, axis=0, keepdims=True) * (-0.5 * scale)
        parts = three_parts(norm)
        aug[:, here] = jnp.concatenate(
            [first, second, first, second, third, first, *parts, jnp.zeros((LANES - 21, LANES), F32)],
            axis=0,
        ).astype(BF16)
        one = jnp.ones((1, LANES), F32)
        gap = jnp.zeros((5, LANES), F32)
        tile = jnp.concatenate(
            [first, one, gap[:4], second, gap, third, gap, jnp.zeros((8, LANES), F32)], axis=0
        )
        x_cols[at * LANES : (at + 1) * LANES, :] = jnp.concatenate(
            [tile.T, jnp.zeros((LANES, LANES - 32), F32)], axis=1
        ).astype(BF16)


def score_all(src_own, src_other, tgt_own, tgt_other, cols, aug, x_cols, state, left, score, highest, *, chunk, tile):
    points = cols.shape[0]
    blocks = points // LANES
    cands = aug.shape[1]
    half = src_own.shape[0]
    for at in range(blocks):
        down = slice(at * LANES, (at + 1) * LANES)
        both = jnp.concatenate([src_own[:, down], src_other[:, down]], axis=0)
        left[down, 0 : 2 * half] = both.T
        left[down, 2 * half :] = cols[down, :].astype(BF16)
    tiles = cands // tile
    per = tile // LANES
    for t in range(tiles):
        across = slice(t * tile, (t + 1) * tile)
        right = jnp.concatenate([tgt_own[:, across], tgt_other[:, across], aug[:, across]], axis=0)
        for r in range(0, points, chunk):
            product = jnp.dot(left[r : r + chunk, :], right, preferred_element_type=F32)
            score[t, r : r + chunk] = product
            top = product[:, :LANES]
            for q in range(1, per):
                top = jnp.maximum(top, product[:, q * LANES : (q + 1) * LANES])
            highest[r : r + chunk] = top if t == 0 else jnp.maximum(highest[r : r + chunk], top)
    ids = lax.broadcasted_iota(jnp.int32, (1, tile), 1).astype(F32)
    state[...] = jnp.zeros_like(state)
    for r in range(0, points, chunk):
        seed = cols[r : r + chunk, 21:22]
        level = cols[r : r + chunk, 22:23]
        top = jnp.max(highest[r : r + chunk], axis=1, keepdims=True) * (feature_scale * LOG2E)
        peak = jnp.maximum(top, level)
        tied = peak - tie_gain * LOG2E
        total = jnp.zeros((chunk, LANES), F32)
        for t in range(tiles):
            shift = jnp.where(ids + float(t * tile) == seed, tied, peak)
            weight = jnp.exp2(score[t, r : r + chunk] * (feature_scale * LOG2E) - shift)
            x = x_cols[t * tile : (t + 1) * tile, :]
            total += jnp.dot(weight.astype(BF16), x, preferred_element_type=F32)
        total = jnp.where(lane_ids() == 4, peak, total)
        highest[r : r + chunk] = total
    for at in range(blocks):
        flat = highest[at * LANES : (at + 1) * LANES, :].T
        summed = flat[0:8] + flat[8:16] + flat[16:24]
        for q in range(5):
            state[q * blocks + at : q * blocks + at + 1, :] = summed[q : q + 1, :]


def slot_ids(slots, blocks):
    rows = lax.broadcasted_iota(jnp.int32, (blocks, LANES), 0)
    return first_slot(slots) + LANES * rows + lane_ids(blocks)


def own_kernel(bundle, out, geo_out):
    blocks = out.shape[1]
    at_z, at_geo, end = bundle_places(blocks)
    geo_out[...] = bundle[at_geo:end, :].astype(BF16)
    for q in range(5):
        out[q] = bundle[q * blocks : (q + 1) * blocks, :]
    z = [bundle[at_z + c * blocks : at_z + (c + 1) * blocks, :] for c in range(3)]
    sigma = bundle[at_z + 4 * blocks : at_z + 5 * blocks, :]
    for c in range(3):
        out[5 + c] = z[c]
    norm = (z[0] * z[0] + z[1] * z[1] + z[2] * z[2]) * (0.5 / sigma)
    out[8] = (norm + outlier_level) * LOG2E
    out[9] = bundle[at_z + 3 * blocks : at_z + 4 * blocks, :]
    out[10] = sigma


def merge_kernel(own, *refs):
    *others, terms, mass_out = refs
    blocks = own.shape[1]
    states = [[own[q] for q in range(5)]]
    for ref in others:
        states.append([ref[q * blocks : (q + 1) * blocks, :] for q in range(5)])
    peak = states[0][4]
    for state in states[1:]:
        peak = jnp.maximum(peak, state[4])
    sums = [jnp.zeros((blocks, LANES), F32)] * 4
    for state in states:
        factor = jnp.exp2(state[4] - peak)
        sums = [s + state[q] * factor for q, s in enumerate(sums)]
    denom = sums[3] + jnp.exp2(own[8] - peak)
    each = own[9] / denom
    mass = sums[3] * each
    inverse = 1.0 / (mass + coherence * own[10])
    terms[...] = jnp.zeros_like(terms)
    for c in range(3):
        terms[c * blocks : (c + 1) * blocks, :] = (sums[c] * each - mass * own[5 + c]) * inverse
    terms[3 * blocks : 4 * blocks, :] = mass * inverse
    mass_out[...] = mass


def to_windows(rows, put):
    lane = lane_ids()
    groups = ROWS_WIN // 4
    for w, begin in enumerate((-REACH, KEEP - REACH, 2 * KEEP - REACH, 3 * KEEP - REACH)):
        row = begin // LANES
        start = begin - row * LANES
        first = rows[pl.ds(8 + row, groups, stride=3), :]
        second = rows[pl.ds(9 + row, groups, stride=3), :]
        put(w, pltpu.roll(jnp.where(lane >= start, first, second), LANES - start, 1))


def fill_rows(rows, values):
    blocks = values.shape[0]
    rows[8 : 8 + blocks, :] = values


def pick(value, index):
    return jnp.take_along_axis(value, index, axis=1, mode="promise_in_bounds")


def each_strip(count, body):
    if count <= 4:
        for j in range(count):
            body(j)
    else:
        lax.fori_loop(0, count, lambda j, c: (body(j), c)[1], 0)


def packed(values):
    first, second, third = (value.astype(jnp.int32) for value in values)
    third = third + (1 << 20)
    return (first << 11) + (third >> 10), (second << 11) + (third & 1023)


def unpacked(words):
    first, second = words
    third = ((first & 2047) << 10) + (second & 1023) - (1 << 20)
    return [value.astype(F32) for value in (first >> 11, second >> 11, third)]


def picked(words, index, later, last, ends):
    low, high = ends
    got = []
    for w in range(len(words[1])):
        value = pick(words[1][w], index)
        if not low:
            value = jnp.where(later, value, pick(words[0][w], index))
        if not high:
            value = jnp.where(last, pick(words[2][w], index), value)
        got.append(value)
    return got


def ends_of(j, strips):
    return (j == 0, j == strips - 1) if isinstance(j, int) else (False, False)


def kernels_kernel(*refs, strips, blocks):
    geos = refs[:strips]
    index_out, segment_out, weight_out, wide, rows, codes, raw, places = refs[strips:]
    groups = ROWS_WIN // 4
    lane = lane_ids(8)
    rows[...] = jnp.zeros_like(rows)
    places[0] = jnp.zeros_like(places[0])
    places[strips + 1] = jnp.zeros_like(places[0])
    unit = float(1 << 19)

    for d in range(strips):
        wide[...] = geos[d][...].astype(F32)
        j = lax.rem(lax.axis_index("strip") + strips - d, strips)

        for k in range(EDGES):
            fill_rows(rows, wide[k * blocks : (k + 1) * blocks, :])

            def put_code(w, value, k=k, j=j):
                codes[j, k, pl.ds(w, groups, stride=4), :] = value

            to_windows(rows, put_code)
        for c in range(3):
            at = (EDGES + c) * blocks
            more = at + 3 * blocks
            fill_rows(rows, wide[at : at + blocks, :] + wide[more : more + blocks, :])

            def put_place(w, value, c=c):
                raw[c, pl.ds(w, groups, stride=4), :] = value

            to_windows(rows, put_place)
        for q, word in enumerate(packed([raw[c] * unit for c in range(3)])):
            places[j + 1, q] = word

    def one_strip(j):
        ends = ends_of(j, strips)
        for v in range(ROWS_WIN // 8):
            down = slice(8 * v, 8 * v + 8)
            near = [[places[j + g, q, down, :] for q in range(2)] for g in range(3)]
            own = unpacked(near[1])
            for k in range(EDGES):
                code = codes[j, k, down, :].astype(jnp.int32)
                later = code >= SPAN
                last = code >= 2 * SPAN
                segment = later.astype(jnp.int32) + last.astype(jnp.int32)
                index = jnp.clip(lane + code - segment * SPAN - REACH, 0, LANES - 1)
                got = unpacked(picked(near, index, later, last, ends))
                gaps = [(own[c] - got[c]) * (1.0 / unit) for c in range(3)]
                gaps[0] = gaps[0] - strip_offset * (segment - 1).astype(F32)
                total = gaps[0] * gaps[0] + gaps[1] * gaps[1] + gaps[2] * gaps[2]
                weight_out[j, k, down, :] = jnp.exp(total * (-0.5 / kernel_scale)) * (1.0 / EDGES)
                index_out[j, k, down, :] = index
                segment_out[j, k, down, :] = segment

    each_strip(strips, one_strip)


FIELD_UNIT = float(1 << 20) / 17.5


def sweep_kernel(*refs, strips, blocks):
    terms = refs[:strips]
    index, segment, weight, disp, _, out = refs[strips : strips + 6]
    rows, base, raw, field, last_rows = refs[strips + 6 :]
    me = lax.axis_index("strip")
    core = lax.axis_index("feat")
    groups = ROWS_WIN // 4
    parts = ROWS_WIN // 8
    lane = lane_ids(8)
    rows[...] = jnp.zeros_like(rows)
    raw[...] = jnp.zeros_like(raw)
    field[0] = jnp.zeros_like(field[0])
    field[strips + 1] = jnp.zeros_like(field[0])

    for d in range(strips):
        j = lax.rem(lax.axis_index("strip") + strips - d, strips)
        for q in range(4):
            fill_rows(rows, terms[d][q * blocks : (q + 1) * blocks, :])

            def put(w, value, q=q, j=j):
                base[j, q, pl.ds(w, groups, stride=4), :] = value

            to_windows(rows, put)
        words = packed([base[j, c] * FIELD_UNIT for c in range(3)])
        for q in range(2):
            field[j + 1, q] = words[q]

    def spread(j, v):
        down = slice(8 * v, 8 * v + 8)
        ends = ends_of(j, strips)
        near = [[field[j + g, q, down, :] for q in range(2)] for g in range(3)]
        sums = [jnp.zeros((8, LANES), F32)] * 3
        for k in range(EDGES):
            part = segment[j, k, down, :]
            got = unpacked(picked(near, index[j, k, down, :], part >= 1, part >= 2, ends))
            size = weight[j, k, down, :]
            sums = [s + size * g for s, g in zip(sums, got)]
        return [s * (1.0 / FIELD_UNIT) for s in sums]

    beyond = jnp.where(lane < LANES // 2, lane + KEEP, lane - KEEP) & (LANES - 1)

    def renew(j):
        for v in range(parts):
            for q in range(2):
                at = 8 * v + 8
                before = raw[j, q, at - 1 : at + 7, :]
                behind = raw[j, q, at + 1 : at + 9, :]
                margin = pick(jnp.where(lane < LANES // 2, behind, before), beyond)
                kept = (lane >= REACH) & (lane < LANES - REACH)
                field[j + 1, q, 8 * v : 8 * v + 8, :] = jnp.where(kept, raw[j, q, at : at + 8, :], margin)

    for sweep in range(SWEEPS):
        wanted = SWEEPS - sweep

        def one_strip(j, wanted=wanted):
            for v in range(parts):
                down = slice(8 * v, 8 * v + 8)
                sums = spread(j, v)
                fresh = [base[j, c, down, :] - base[j, 3, down, :] * sums[c] for c in range(3)]
                words = packed([value * FIELD_UNIT for value in fresh])
                for q in range(2):
                    raw[j, q, 8 * v + 8 : 8 * v + 16, :] = words[q]
                if wanted == 1:

                    @pl.when(me == j)
                    def _():
                        for c in range(3):
                            last_rows[c, down, :] = fresh[c]

        def near_strip(j, body, wanted=wanted):
            if strips <= 4 and wanted > 1:
                body(j)
            else:
                pl.when(jnp.abs(me - j) <= wanted)(lambda: body(j))

        each_strip(strips, lambda j: near_strip(j, one_strip))
        each_strip(strips, lambda j: near_strip(j, renew))

    for v in range(parts):
        down = slice(8 * v, 8 * v + 8)
        sums = spread(me, v)
        for c in range(3):
            last_rows[c, down, :] = sums[c] + last_rows[c, down, :]
    wide_lane = lane_ids()
    live = disp[3] > 0.5
    for c in range(3):
        for i in range(3):
            begin = LANES * i - KEEP * i + REACH
            first = last_rows[c, pl.ds(i, groups, stride=4), :]
            second = last_rows[c, pl.ds(i + 1, groups, stride=4), :]
            held = KEEP - (LANES - KEEP) * i
            value = jnp.where(
                wide_lane < held,
                pltpu.roll(first, LANES - begin, 1),
                pltpu.roll(second, (held - REACH) % LANES, 1),
            )
            rows[pl.ds(i, groups, stride=3), :] = value
        rows[0:blocks, :] = disp[c] + jnp.where(live, rows[0:blocks, :], 0.0)
        for at in range(blocks - 1):
            out[c : c + 1, at * LANES : (at + 1) * LANES] = rows[pl.ds(core + at, 1), :]


def takes(microseconds):
    return pl.CostEstimate(flops=int(microseconds * 1.15e9), bytes_accessed=0, transcendentals=0)


def whole_kernel(part, part_far, mass, mass_far, out, mass_out):
    is_first = lax.axis_index("feat") == 0
    blocks = mass.shape[0]
    half = blocks - 1
    wide = part.shape[1]
    out[:, 0:wide] = jnp.where(is_first, part[...], part_far[...])
    out[:, wide:] = jnp.where(is_first, part_far[...], part[...])
    mass_out[0:half, :] = jnp.where(is_first, mass[0:half, :], mass_far[0:half, :])
    mass_out[half:, :] = jnp.where(is_first, mass_far[1:blocks, :], mass[1:blocks, :])


def around(array, axis):
    count = lax.axis_size(axis)
    return [array] + [
        lax.ppermute(array, axis, [(i, (i + d) % count) for i in range(count)]) for d in range(1, count)
    ]


def on_device(
    src_pos, src_feat, tgt_pos, tgt_feat, displacement, sigma_sq, seed_target, counts, edges
):
    slots = src_pos.shape[1]
    cands = tgt_pos.shape[1]
    strips = lax.axis_size("strip")
    half = slots // 2
    points = half + LANES
    blocks = points // LANES
    small = pltpu.CompilerParams(vmem_limit_bytes=12 << 20)

    src_other = around(src_feat, "feat")[1]
    tgt_other = around(tgt_feat, "feat")[1]

    geo_rows = 16 * ((14 * blocks + 15) // 16)
    hbm = pl.BlockSpec(memory_space=pltpu.HBM)
    held = pl.pallas_call(
        hold_kernel,
        name="hold",
        out_shape=jax.ShapeDtypeStruct((8, LANES), F32),
        out_specs=VMEM,
        compiler_params=pltpu.CompilerParams(vmem_limit_bytes=(64 << 20) - (64 << 10)),
        cost_estimate=takes(2),
    )()
    arrays = (src_pos, displacement, tgt_pos, seed_target.reshape(1, slots), edges)
    features = (src_feat, src_other, tgt_feat, tgt_other)
    tile = 256
    state_rows = 8 * ((5 * blocks + 7) // 8)
    mine = pltpu.VMEM((src_feat.shape[0], points), BF16)
    theirs = pltpu.VMEM(tgt_feat.shape, BF16)
    state, bundle, disp = pl.pallas_call(
        functools.partial(score_kernel, chunk=points // 8, tile=tile),
        name="score",
        out_shape=(
            jax.ShapeDtypeStruct((state_rows, LANES), F32),
            jax.ShapeDtypeStruct((bundle_places(blocks)[2], LANES), F32),
            jax.ShapeDtypeStruct((4, blocks, LANES), F32),
        ),
        in_specs=[hbm] * 11 + [pl.BlockSpec(memory_space=pl.ANY)],
        out_specs=(VMEM,) * 3,
        scratch_shapes=[pltpu.SMEM((1,), F32)]
        + [pltpu.VMEM(array.shape, array.dtype) for array in arrays]
        + [pltpu.SMEM((1,), jnp.int32)]
        + [mine, mine, theirs, theirs]
        + [
            pltpu.VMEM((points, LANES), F32),
            pltpu.VMEM((LANES, cands), BF16),
            pltpu.VMEM((cands, LANES), BF16),
            pltpu.VMEM((points, 2 * LANES), BF16),
            pltpu.VMEM((cands // tile, points, tile), F32),
            pltpu.VMEM((points, LANES), F32),
            pltpu.SemaphoreType.DMA((11,)),
        ],
        compiler_params=pltpu.CompilerParams(vmem_limit_bytes=60 << 20),
        cost_estimate=takes(10),
    )(sigma_sq, *arrays, counts, *features, held)

    own, geo = pl.pallas_call(
        own_kernel,
        name="own",
        out_shape=(
            jax.ShapeDtypeStruct((11, blocks, LANES), F32),
            jax.ShapeDtypeStruct((geo_rows, LANES), BF16),
        ),
        in_specs=[VMEM],
        out_specs=(VMEM, VMEM),
        compiler_params=small,
        cost_estimate=takes(0.5),
    )(bundle)
    geos = around(geo, "strip")
    shape = (strips, EDGES, ROWS_WIN, LANES)
    index, segment, weight = pl.pallas_call(
        functools.partial(kernels_kernel, strips=strips, blocks=blocks),
        name="neighbours",
        out_shape=(
            jax.ShapeDtypeStruct(shape, jnp.int32),
            jax.ShapeDtypeStruct(shape, jnp.int32),
            jax.ShapeDtypeStruct(shape, F32),
        ),
        in_specs=[VMEM] * strips,
        out_specs=(VMEM,) * 3,
        scratch_shapes=[
            pltpu.VMEM((geo_rows, LANES), F32),
            pltpu.VMEM((ROWS_WIN + 16, LANES), F32),
            pltpu.VMEM(shape, F32),
            pltpu.VMEM((3, ROWS_WIN, LANES), F32),
            pltpu.VMEM((strips + 2, 2, ROWS_WIN, LANES), jnp.int32),
        ],
        compiler_params=small,
        cost_estimate=takes(2),
    )(*geos)

    states = around(state, "cand")
    term_rows = 8 * ((4 * blocks + 7) // 8)
    terms, mass = pl.pallas_call(
        merge_kernel,
        name="merge",
        out_shape=(
            jax.ShapeDtypeStruct((term_rows, LANES), F32),
            jax.ShapeDtypeStruct((blocks, LANES), F32),
        ),
        in_specs=[VMEM] * len(states),
        out_specs=(VMEM, VMEM),
        compiler_params=small,
        cost_estimate=takes(0.5),
    )(own, *states[1:])

    all_terms = around(terms, "strip")
    mass_far = around(mass, "feat")[1]

    part = pl.pallas_call(
        functools.partial(sweep_kernel, strips=strips, blocks=blocks),
        name="sweeps",
        out_shape=jax.ShapeDtypeStruct((3, half), F32),
        in_specs=[VMEM] * (strips + 4) + [pl.BlockSpec(memory_space=pl.ANY)],
        out_specs=VMEM,
        scratch_shapes=[
            pltpu.VMEM((ROWS_WIN + 16, LANES), F32),
            pltpu.VMEM((strips, 4, ROWS_WIN, LANES), F32),
            pltpu.VMEM((strips, 2, ROWS_WIN + 16, LANES), jnp.int32),
            pltpu.VMEM((strips + 2, 2, ROWS_WIN, LANES), jnp.int32),
            pltpu.VMEM((3, ROWS_WIN + 8, LANES), F32),
        ],
        compiler_params=small,
        cost_estimate=takes(7),
    )(*all_terms, index, segment, weight, disp, mass_far)

    new_disp, mass_whole = pl.pallas_call(
        whole_kernel,
        name="whole",
        out_shape=(
            jax.ShapeDtypeStruct((3, slots), F32),
            jax.ShapeDtypeStruct((slots // LANES, LANES), F32),
        ),
        in_specs=[VMEM] * 4,
        out_specs=(VMEM, VMEM),
        compiler_params=small,
        cost_estimate=takes(0.5),
    )(part, around(part, "feat")[1], mass, mass_far)
    return (new_disp, mass_whole.reshape(slots))


def solution(mesh):
    in_specs = (
        P(None, ("groups", "strip")),
        P("feat", ("groups", "strip")),
        P(None, ("groups", "strip", "cand")),
        P("feat", ("groups", "strip", "cand")),
        P(None, ("groups", "strip")),
        P(("groups", "strip")),
        P(("groups", "strip")),
        P(("groups", "strip")),
        P(None, ("groups", "strip")),
    )
    out_specs = (P(None, ("groups", "strip")), P(("groups", "strip")))
    return jax.shard_map(
        on_device, mesh=mesh, in_specs=in_specs, out_specs=out_specs, check_vma=False
    )
```
